32 devices in a mesh: dp: 4 (over y, x), ctx: 8 (over z, core).
Axes of the slice: x: 2, y: 2, z: 4, core: 2. Of those that a mesh axis runs over, the one named last changes fastest.
Arguments:
- tokens: bfloat16 [4, 4096, 1024], P('dp', 'ctx'), may hold values from -6 to 6
- starts: int32 [4, 512], P('dp', 'ctx'), may hold values from 0 to 4095, as said below
- gain: float32 [1024], replicated, may hold values from 0.1 to 1.9
- w_query: bfloat16 [1024, 1024], P('dp')
- w_key: bfloat16 [1024, 1024], P('dp')
- w_value: bfloat16 [1024, 1024], P('dp'), may hold values from -0.1875 to 0.1875
- w_out: bfloat16 [1024, 1024], P('dp'), may hold values from -0.1875 to 0.1875
- cotangent: bfloat16 [4, 4096, 1024], P('dp', 'ctx'), may hold values from -6 to 6
Outputs:
- grad_tokens: bfloat16 [4, 4096, 1024], P('dp', 'ctx')
The draws below stay inside these ranges and needn't reach their ends.
Inputs may be any that keep to these rules, and one draw needn't show every extreme that they name: starts[b, 0] is 0 and starts[b, j] rises strictly with j; segment j lies with the device that holds starts[b, j], and every position held by one device along ctx belongs to a segment held by that device or by one of its two neighbours along ctx; in the first sequence segment 64 - 1 starts at 513 or later and the last segment starts at 4095.
All inputs are finite; a program needn't handle non-finite values.
Results may differ from the reference program's by a relative error of at most 0.013.
Values may be sent and summed in bfloat16 or wider, within the bound.
A program may use at most 128 MiB of HBM per device.

```python
import math
import jax
import jax.numpy as jnp
from jax import lax

D = 1024
HEADS = 8
HEAD = 128
SHORTEN = 8
TOK_DEV = 512
BATCH = 4
LENGTH = 4096
SEG_DEV = 64
SEGS = 512


def draw_starts(key, part):
    key = jax.random.fold_in(key, 3)
    first_key, second_key = jax.random.split(key)
    upper = 2 * SHORTEN - 1
    first_draw = jax.random.randint(first_key, (BATCH, SEGS), 0, upper)
    second_draw = jax.random.randint(second_key, (BATCH, SEGS), 0, upper)
    index = jnp.arange(SEGS, dtype=jnp.int32)[None, :]
    row = jnp.arange(BATCH, dtype=jnp.int32)[:, None]
    length = 1 + first_draw * second_draw // (2 * SHORTEN - 2)
    stride = jnp.where(index == 0, 0, length - SHORTEN)
    walk = jnp.cumsum(stride, axis=1).astype(jnp.int32)
    drift = TOK_DEV // 2
    folded = jnp.mod(walk + drift, 4 * drift)
    folded = jnp.where(folded <= 2 * drift, folded, 4 * drift - folded)
    offset = folded - drift
    raw = index * SHORTEN + offset
    ceiling = LENGTH - (SEGS - index)
    result = jnp.maximum(index, jnp.minimum(raw, ceiling))
    pivot = SEG_DEV - 1
    below = (row == 0) & (index < pivot)
    above = (row == 0) & (index >= pivot)
    result = jnp.where(below, jnp.minimum(result, TOK_DEV + 1 - (pivot - index)), result)
    result = jnp.where(above, jnp.maximum(result, TOK_DEV + 1 + (index - pivot)), result)
    result = jnp.where((index == SEGS - 1) & (row == 0), LENGTH - 1, result)
    return result.astype(jnp.int32)


def draw_w_query(key, part):
    key = jax.random.fold_in(key, 5)
    own = jax.random.normal(key, (D, HEADS * HEAD), jnp.float32)
    result = own / math.sqrt(D)
    return result.astype(jnp.bfloat16)


def draw_w_key(key, part):
    key = jax.random.fold_in(key, 7)
    own = jax.random.normal(key, (D, HEADS * HEAD), jnp.float32)
    result = own / math.sqrt(D)
    return result.astype(jnp.bfloat16)


def block_scale(key, shape, pieces, low, largest):
    loudness, own = 1.0, jax.random.fold_in(key, 6)
    for axis_at, parts in pieces:
        steps = jnp.exp(jax.random.uniform(jax.random.fold_in(own, axis_at), (parts,), jnp.float32, low / len(pieces), largest / len(pieces)))
        loudness = loudness * jnp.repeat(steps, shape[axis_at] // parts).reshape([-1 if axis == axis_at else 1 for axis in range(len(shape))])
    return loudness


def normal_values(stream_key, shape, scale, reach, pieces=(), kind=jnp.bfloat16):
    loudness = block_scale(stream_key, shape, pieces, -0.22, 0.18) if pieces else 1.0
    values = jax.random.normal(stream_key, shape, jnp.float32) * scale * loudness
    return jnp.minimum(jnp.maximum(values, -reach), reach).astype(kind)


def setup_inputs(seed: int = 0) -> dict:
    streams_of = jax.random.split(jax.random.key(seed), 9)
    return {
        "tokens": normal_values(streams_of[0], (BATCH, LENGTH, D), 1.0, 6.0, ((0, 4), (1, 8))),
        "starts": draw_starts(jax.random.fold_in(streams_of[8], 71), 0),
        "gain": jnp.clip(1.0 + 0.18 * jax.random.normal(streams_of[2], (D,), jnp.float32), 0.1, 1.9),
        "w_query": draw_w_query(jax.random.fold_in(streams_of[8], 71), 0),
        "w_key": draw_w_key(jax.random.fold_in(streams_of[8], 71), 0),
        "w_value": normal_values(streams_of[5], (D, HEADS * HEAD), D ** -0.5, 0.1875, ((0, 4),)),
        "w_out": normal_values(streams_of[6], (HEADS * HEAD, D), (HEADS * HEAD) ** -0.5, 0.1875, ((0, 4),)),
        "cotangent": normal_values(streams_of[7], (BATCH, LENGTH, D), 1.0, 6.0, ((0, 4), (1, 8))),
    }


def reference(tokens, starts, gain, w_query, w_key, w_value, w_out, cotangent):
    inner = HEADS * HEAD
    scale = 1.0 / math.sqrt(HEAD)

    def one_sequence(items):
        xrow, first_pos, grad_out = items
        positions = jnp.arange(LENGTH, dtype=jnp.int32)
        seg = (jnp.searchsorted(first_pos, positions, side='right') - 1).astype(jnp.int32)
        count = jax.ops.segment_sum(jnp.ones((LENGTH,), jnp.float32), seg, num_segments=SEGS)
        pooled = jax.ops.segment_sum(xrow.astype(jnp.float32), seg, num_segments=SEGS) / count[:, None]
        rms = jnp.sqrt(lax.optimization_barrier(jnp.mean(pooled * pooled, axis=-1, keepdims=True)) + 1e-06)
        normed = pooled / rms
        normin = (normed * gain).astype(jnp.bfloat16)
        query = jnp.dot(normin, w_query, preferred_element_type=jnp.float32).astype(jnp.bfloat16).reshape(SEGS, HEADS, HEAD)
        keys = jnp.dot(normin, w_key, preferred_element_type=jnp.float32).astype(jnp.bfloat16).reshape(SEGS, HEADS, HEAD)
        values = jnp.dot(normin, w_value, preferred_element_type=jnp.float32).astype(jnp.bfloat16).reshape(SEGS, HEADS, HEAD)
        allowed = jnp.arange(SEGS)[None, :] <= jnp.arange(SEGS)[:, None]
        score = jnp.einsum('qhd,khd->hqk', query.astype(jnp.float32), keys.astype(jnp.float32)) * scale
        score = jnp.where(allowed[None], score, -1e+30)
        peak = lax.optimization_barrier(jnp.max(score, axis=-1, keepdims=True))
        expo = jnp.where(allowed[None], jnp.exp(score - peak), 0.0)
        probs = expo / lax.optimization_barrier(jnp.sum(expo, axis=-1, keepdims=True))
        probs_b = probs.astype(jnp.bfloat16)
        attended = jnp.einsum('hqk,khd->qhd', probs_b.astype(jnp.float32), values.astype(jnp.float32)).astype(jnp.bfloat16)
        earlier = jnp.where(seg > 0, seg - 1, SEGS).astype(jnp.int32)
        dout = jax.ops.segment_sum(grad_out.astype(jnp.float32), earlier, num_segments=SEGS + 1)[:SEGS]
        dout_b = dout.astype(jnp.bfloat16)
        dattended = jnp.dot(dout_b, w_out.T, preferred_element_type=jnp.float32).astype(jnp.bfloat16).reshape(SEGS, HEADS, HEAD)
        delta = jnp.einsum('qhd,qhd->hq', dattended.astype(jnp.float32), attended.astype(jnp.float32))
        dprobs = jnp.einsum('qhd,khd->hqk', dattended.astype(jnp.float32), values.astype(jnp.float32))
        dscore = (probs * (dprobs - delta[:, :, None])).astype(jnp.bfloat16)
        dquery = (jnp.einsum('hqk,khd->qhd', dscore.astype(jnp.float32), keys.astype(jnp.float32)) * scale).astype(jnp.bfloat16).reshape(SEGS, inner)
        dkey = (jnp.einsum('hqk,qhd->khd', dscore.astype(jnp.float32), query.astype(jnp.float32)) * scale).astype(jnp.bfloat16).reshape(SEGS, inner)
        dvalue = jnp.einsum('hqk,qhd->khd', probs_b.astype(jnp.float32), dattended.astype(jnp.float32)).astype(jnp.bfloat16).reshape(SEGS, inner)
        dnormin = jnp.dot(dquery, w_query.T, preferred_element_type=jnp.float32)
        dnormin = dnormin + jnp.dot(dkey, w_key.T, preferred_element_type=jnp.float32)
        dnormin = dnormin + jnp.dot(dvalue, w_value.T, preferred_element_type=jnp.float32)
        scaled = dnormin * gain
        dpooled = dout + (scaled - normed * lax.optimization_barrier(jnp.mean(scaled * normed, axis=-1, keepdims=True))) / rms
        per_seg = dpooled / count[:, None]
        return (grad_out.astype(jnp.float32) + per_seg[seg]).astype(jnp.bfloat16)
    return lax.map(one_sequence, (tokens, starts, cotangent))
```

```python
import functools
import math

import jax
import jax.numpy as jnp
from jax import lax
from jax.experimental import pallas as pl
from jax.experimental.pallas import tpu as pltpu
from jax.sharding import PartitionSpec as P

HEAD = 128
BF = jnp.bfloat16
F32 = jnp.float32


def dot(left, right, dims):
    return lax.dot_general(left, right, ((dims[0], dims[1]), ((), ())), preferred_element_type=F32)


def mm(left, right):
    return dot(left, right, ((1,), (0,)))


def mm_nt(left, right):
    return dot(left, right, ((1,), (1,)))


def mm_tn(left, right):
    return dot(left, right, ((0,), (0,)))


def remote(src, dst, send, recv, **where):
    return pltpu.make_async_remote_copy(
        src_ref=src, dst_ref=dst, send_sem=send, recv_sem=recv,
        device_id=where, device_id_type=pl.DeviceIdType.MESH,
    )


def kernel(
    n, dp,
    tok, starts, gain, wq, wk, wv, wo, cot, out,
    st_mine, st_near, near_out, near_in, gath, wcat, wout, qkv, datt, dqkv, dkv,
    part, sib, red, rs, seg_out, seg_in, member_s,
    st_send, st_recv, near_send, near_recv, seg_send, seg_recv,
    w_send, w_recv, w_local, wo_send, wo_recv, wo_local,
    right_send, left_send, pair_send, gath_recv, sib_send, sib_recv, rs_send, rs_recv,
):
    me = lax.axis_index("dp")
    c = lax.axis_index("ctx")
    core = lax.rem(c, 2)
    chip = lax.div(c, 2)
    chips = n // 2
    mate = c + 1 - 2 * core
    rows = tok.shape[1]
    width = tok.shape[2]
    seg_dev = starts.shape[1]
    segs = n * seg_dev
    w_rows = wq.shape[0]
    inner = wq.shape[1]
    heads = inner // HEAD
    parts = n // heads
    h = lax.rem(c, heads)
    r = lax.div(c, heads)
    scale = 1.0 / math.sqrt(HEAD)
    has_prev, has_next = c > 0, c < n - 1

    barrier = pltpu.get_barrier_semaphore()
    for o in range(1, n):
        pl.semaphore_signal(barrier, inc=1, device_id={"ctx": lax.rem(c + o, n)},
                            device_id_type=pl.DeviceIdType.MESH)
    for o in range(1, dp):
        pl.semaphore_signal(barrier, inc=1, device_id={"dp": lax.rem(me + o, dp)},
                            device_id_type=pl.DeviceIdType.MESH)
    st_mine[...] = jnp.zeros_like(st_mine)
    st_mine[0:1, 0:seg_dev] = starts[...]
    pl.semaphore_wait(barrier, n - 1 + dp - 1)

    def to_next(src, dst, send, recv):
        return remote(src, dst.at[0], send.at[0], recv.at[0], ctx=c + 1)

    def to_prev(src, dst, send, recv):
        return remote(src, dst.at[1], send.at[1], recv.at[1], ctx=c - 1)

    def near_start(src_next, src_prev, dst, send, recv):
        @pl.when(has_next)
        def _():
            to_next(src_next, dst, send, recv).start()

        @pl.when(has_prev)
        def _():
            to_prev(src_prev, dst, send, recv).start()

    def near_wait(src_next, src_prev, dst, send, recv):
        @pl.when(has_prev)
        def _():
            to_next(src_next, dst, send, recv).wait_recv()
            to_prev(src_prev, dst, send, recv).wait_send()

        @pl.when(has_next)
        def _():
            to_prev(src_prev, dst, send, recv).wait_recv()
            to_next(src_next, dst, send, recv).wait_send()

    near_start(st_mine, st_mine, st_near, st_send, st_recv)

    head_at = pl.multiple_of(h * HEAD, HEAD)
    mats = (wq, wk, wv)

    def w_copy(o, i):
        mine = pl.ds(pl.multiple_of(me * w_rows, w_rows), w_rows)
        return remote(mats[i].at[:, pl.ds(head_at, HEAD)], wcat.at[mine, pl.ds(i * HEAD, HEAD)],
                      w_send.at[o - 1, i], w_recv.at[o - 1, i], dp=lax.rem(me + o, dp))

    def w_arrival(o, i):
        src = lax.rem(me + dp - o, dp)
        theirs = pl.ds(pl.multiple_of(src * w_rows, w_rows), w_rows)
        return remote(mats[i].at[:, pl.ds(head_at, HEAD)], wcat.at[theirs, pl.ds(i * HEAD, HEAD)],
                      w_send.at[o - 1, i], w_recv.at[o - 1, i], dp=lax.rem(me + o, dp))

    def w_own(i):
        mine = pl.ds(pl.multiple_of(me * w_rows, w_rows), w_rows)
        return pltpu.make_async_copy(mats[i].at[:, pl.ds(head_at, HEAD)],
                                     wcat.at[mine, pl.ds(i * HEAD, HEAD)], w_local.at[i])

    holder = lax.div(h * HEAD, w_rows)
    holder_at = pl.ds(pl.multiple_of(lax.rem(h * HEAD, w_rows), HEAD), HEAD)

    def wo_copy(o):
        return remote(wo.at[holder_at], wout, wo_send.at[o - 1], wo_recv.at[0],
                      dp=lax.rem(me + o, dp))

    for o in range(1, dp):
        for i in range(3):
            w_copy(o, i).start()
    for i in range(3):
        w_own(i).start()

    @pl.when(me == holder)
    def _():
        for o in range(1, dp):
            wo_copy(o).start()
        pltpu.make_async_copy(wo.at[holder_at], wout, wo_local.at[0]).start()

    near_wait(st_mine, st_mine, st_near, st_send, st_recv)
    own_row = starts[...].astype(F32)
    prev_row = jnp.where(has_prev, st_near[0, 0:1, 0:seg_dev].astype(F32), -1.0)
    next_row = jnp.where(has_next, st_near[1, 0:1, 0:seg_dev].astype(F32), float(rows * n))
    sub = lax.broadcasted_iota(jnp.int32, (seg_dev, seg_dev), 0)
    lane = lax.broadcasted_iota(jnp.int32, (seg_dev, seg_dev), 1)

    def column(mask, row):
        return jnp.sum(jnp.where(mask, row, 0.0), axis=1, keepdims=True)

    def follow(row, after):
        edge = (sub == seg_dev - 1) & (lane == 0)
        return column(lane == sub + 1, row) + column(edge, after)

    same = lane == sub
    pos = (lax.broadcasted_iota(jnp.int32, (1, rows), 1) + c * rows).astype(F32)
    own_col, own_end = column(same, own_row), follow(own_row, next_row)
    end_row = jnp.full((1, seg_dev), float(rows * n), F32)

    def belongs(first, last):
        return jnp.where((first <= pos) & (pos < last), 1.0, 0.0).astype(BF)

    member_s[0:seg_dev] = belongs(column(same, prev_row), follow(prev_row, own_row))
    member_s[seg_dev:2 * seg_dev] = belongs(own_col, own_end)
    member_s[2 * seg_dev:] = belongs(column(same, next_row), follow(next_row, end_row))

    for side, at in ((1, 0), (0, 2 * seg_dev)):
        some = member_s[at:at + seg_dev]
        near_out[side, :, 0:width] = mm(some, tok[0]).astype(BF)
        near_out[side, :, width:] = mm(some, cot[0]).astype(BF)
    near_start(near_out.at[0], near_out.at[1], near_in, near_send, near_recv)
    some = member_s[seg_dev:2 * seg_dev]
    sum_tok = mm(some, tok[0])
    sum_cot = mm(some, cot[0])

    @pl.when(jnp.logical_not(has_prev))
    def _():
        near_in[0] = jnp.zeros_like(near_in[0])

    @pl.when(jnp.logical_not(has_next))
    def _():
        near_in[1] = jnp.zeros_like(near_in[1])

    near_wait(near_out.at[0], near_out.at[1], near_in, near_send, near_recv)

    def spot(k, where):
        return gath.at[k, pl.ds(pl.multiple_of(where * seg_dev, seg_dev), seg_dev)]

    def hop(k, src_chip, sems, **where):
        at = 2 * src_chip + core
        return remote(spot(k, at), spot(k, at), sems.at[k, src_chip], gath_recv.at[k, at], **where)

    def go_right(k, src):
        return hop(k, src, right_send, ctx=c + 2)

    def go_left(k, src):
        return hop(k, src, left_send, ctx=c - 2)

    def go_pair(k, src):
        return hop(k, src, pair_send, ctx=mate)

    def arrival(k, where):
        return remote(spot(k, where), spot(k, where), right_send.at[k, 0], gath_recv.at[k, where],
                      ctx=mate)

    not_last, not_first = chip < chips - 1, chip > 0

    def launch(k):
        @pl.when(not_last)
        def _():
            go_right(k, chip).start()

        @pl.when(not_first)
        def _():
            go_left(k, chip).start()

        go_pair(k, chip).start()

    own_at = pl.ds(pl.multiple_of(c * seg_dev, seg_dev), seg_dev)
    grad_sum = sum_cot + near_in[0, :, width:].astype(F32) + near_in[1, :, width:].astype(F32)
    gath[0, own_at] = grad_sum.astype(BF)
    launch(0)
    count = own_end - own_col
    pooled = (sum_tok + near_in[0, :, 0:width].astype(F32) + near_in[1, :, 0:width].astype(F32)) / count
    rms = jnp.sqrt(jnp.mean(pooled * pooled, axis=-1, keepdims=True) + 1e-06)
    normed = pooled / rms
    gath[1, own_at] = (normed * gain[...]).astype(BF)
    launch(1)

    for s in range(1, chips):
        for k in range(2):
            @pl.when(chip - s >= 0)
            def _():
                arrival(k, c - 2 * s).wait_recv()

                @pl.when(not_last)
                def _():
                    go_right(k, chip - s).start()

                go_pair(k, chip - s).start()

            @pl.when(chip + s < chips)
            def _():
                arrival(k, c + 2 * s).wait_recv()

                @pl.when(not_first)
                def _():
                    go_left(k, chip + s).start()

                go_pair(k, chip + s).start()

    for o in range(1, dp):
        for i in range(3):
            w_arrival(o, i).wait_recv()
    for i in range(3):
        w_own(i).wait()

    @pl.when(me == holder)
    def _():
        pltpu.make_async_copy(wo.at[holder_at], wout, wo_local.at[0]).wait()

    @pl.when(me != holder)
    def _():
        wo_copy(1).wait_recv()

    for k in range(2):
        for other in range(chips):
            arrival(k, 2 * other + 1 - core).wait_recv()

    step = 512 if segs % 512 == 0 else seg_dev

    def project(b, _):
        at = pl.ds(pl.multiple_of(b * step, step), step)
        qkv[at] = mm(gath[1, at], wcat[...]).astype(BF)
        datt[at] = mm_nt(gath[0, at], wout[...])
        return 0

    lax.fori_loop(0, segs // step, project, 0)
    shifted = pltpu.roll(datt[...], segs - 1, 0)
    last = lax.broadcasted_iota(jnp.int32, (segs, HEAD), 0) == segs - 1
    datt[...] = jnp.where(last, 0.0, shifted)

    dkv[...] = jnp.zeros_like(dkv)
    if parts > 1:
        dqkv[...] = jnp.zeros_like(dqkv)
    block = 128

    def attend(q_at, first, klen):
        q = qkv[q_at, 0:HEAD]
        key = qkv[0:klen, HEAD:2 * HEAD]
        value = qkv[0:klen, 2 * HEAD:]
        grad = datt[q_at].astype(BF)
        score = mm_nt(q, key) * scale
        allowed = (lax.broadcasted_iota(jnp.int32, (block, klen), 1)
                   <= lax.broadcasted_iota(jnp.int32, (block, klen), 0) + first)
        score = jnp.where(allowed, score, -1e30)
        peak = jnp.max(score, axis=-1, keepdims=True)
        expo = jnp.where(allowed, jnp.exp(score - peak), 0.0)
        probs = expo / jnp.sum(expo, axis=-1, keepdims=True)
        probs_b = probs.astype(BF)
        attended = mm(probs_b, value).astype(BF).astype(F32)
        delta = jnp.sum(grad.astype(F32) * attended, axis=-1, keepdims=True)
        dscore = (probs * (mm_nt(grad, value) - delta)).astype(BF)
        dqkv[q_at, 0:HEAD] = (mm(dscore, key) * scale).astype(BF)
        dkv[0:klen, 0:HEAD] += mm_tn(dscore, q)
        dkv[0:klen, HEAD:] += mm_tn(probs_b, grad)

    per = segs // parts // block
    if parts == 1:
        for b in range(per):
            attend(slice(b * block, (b + 1) * block), b * block, (b + 1) * block)
    else:
        def body(b, _):
            first = pl.multiple_of((r * per + b) * block, block)
            attend(pl.ds(first, block), first, segs)
            return 0

        lax.fori_loop(0, per, body, 0)
    dqkv[:, HEAD:2 * HEAD] = (dkv[:, 0:HEAD] * scale).astype(BF)
    dqkv[:, 2 * HEAD:] = dkv[:, HEAD:].astype(BF)

    def sib_copy(t):
        return remote(part.at[1 - core, t], sib.at[t], sib_send.at[t], sib_recv.at[t], ctx=mate)

    def rs_copy(t):
        return remote(red.at[t], rs.at[chip], rs_send.at[t], rs_recv.at[chip], ctx=2 * t + core)

    def rs_arrival(t):
        return remote(red.at[t], rs.at[t], rs_send.at[t], rs_recv.at[t], ctx=mate)

    for t in range(chips):
        term = mm_nt(dqkv[2 * t * seg_dev:2 * (t + 1) * seg_dev], wcat[...])
        part[0, t] = term[0:seg_dev].astype(BF)
        part[1, t] = term[seg_dev:].astype(BF)
        sib_copy(t).start()
    for t in range(chips):
        sib_copy(t).wait_recv()
        red[t] = (part[core, t].astype(F32) + sib[t].astype(F32)).astype(BF)

        @pl.when(chip != t)
        def _():
            rs_copy(t).start()
    dnormin = red[chip].astype(F32)
    for o in range(1, chips):
        t = lax.rem(chip + o, chips)
        rs_arrival(t).wait_recv()
        dnormin = dnormin + rs[t].astype(F32)

    after = gath[0, pl.ds(pl.multiple_of(lax.rem(c + 1, n) * seg_dev, seg_dev), seg_dev)].astype(F32)
    tail = jnp.where(has_next, after[0:1], 0.0)
    rolled = pltpu.roll(grad_sum, seg_dev - 1, 0)
    ends = lax.broadcasted_iota(jnp.int32, (seg_dev, width), 0) == seg_dev - 1
    dout = jnp.where(ends, tail, rolled)
    scaled = dnormin * gain[...]
    dpooled = dout + (scaled - normed * jnp.mean(scaled * normed, axis=-1, keepdims=True)) / rms
    seg_out[...] = (dpooled / count).astype(BF)
    near_start(seg_out, seg_out, seg_in, seg_send, seg_recv)

    @pl.when(jnp.logical_not(has_prev))
    def _():
        seg_in[0] = jnp.zeros_like(seg_in[0])

    @pl.when(jnp.logical_not(has_next))
    def _():
        seg_in[1] = jnp.zeros_like(seg_in[1])

    for k in range(2):
        for other in range(chips):
            @pl.when(not_last & (other <= chip))
            def _():
                go_right(k, other).wait_send()

            @pl.when(not_first & (other >= chip))
            def _():
                go_left(k, other).wait_send()

            go_pair(k, other).wait_send()
    for t in range(chips):
        sib_copy(t).wait_send()

        @pl.when(chip != t)
        def _():
            rs_copy(t).wait_send()
    for o in range(1, dp):
        for i in range(3):
            w_copy(o, i).wait_send()

    @pl.when(me == holder)
    def _():
        for o in range(1, dp):
            wo_copy(o).wait_send()

    near_wait(seg_out, seg_out, seg_in, seg_send, seg_recv)
    window = jnp.concatenate([seg_in[0], seg_out[...], seg_in[1]], axis=0)
    spread = mm_tn(member_s[...], window)
    out[0] = (cot[0].astype(F32) + spread).astype(BF)


def per_device(tokens, starts, gain, w_query, w_key, w_value, w_out, cotangent):
    n, dp = lax.axis_size("ctx"), lax.axis_size("dp")
    chips = n // 2
    rows, width = tokens.shape[1:]
    seg_dev = starts.shape[1]
    segs = n * seg_dev
    dma = pltpu.SemaphoreType.DMA
    vmem = pltpu.VMEM
    scratch = [
        vmem((8, 128), jnp.int32),
        vmem((2, 8, 128), jnp.int32),
        vmem((2, seg_dev, 2 * width), BF),
        vmem((2, seg_dev, 2 * width), BF),
        vmem((2, segs, width), BF),
        vmem((width, 3 * HEAD), BF),
        vmem((HEAD, width), BF),
        vmem((segs, 3 * HEAD), BF),
        vmem((segs, HEAD), F32),
        vmem((segs, 3 * HEAD), BF),
        vmem((segs, 2 * HEAD), F32),
        vmem((2, chips, seg_dev, width), BF),
        vmem((chips, seg_dev, width), BF),
        vmem((chips, seg_dev, width), BF),
        vmem((chips, seg_dev, width), BF),
        vmem((seg_dev, width), BF),
        vmem((2, seg_dev, width), BF),
        vmem((3 * seg_dev, rows), BF),
        dma((2,)), dma((2,)), dma((2,)), dma((2,)), dma((2,)), dma((2,)),
        dma((dp - 1, 3)), dma((dp - 1, 3)), dma((3,)), dma((dp - 1,)), dma((1,)), dma((1,)),
        dma((2, chips)), dma((2, chips)), dma((2, chips)), dma((2, n)),
        dma((chips,)), dma((chips,)), dma((chips,)), dma((chips,)),
    ]
    return pl.pallas_call(
        functools.partial(kernel, n, dp),
        out_shape=jax.ShapeDtypeStruct(tokens.shape, BF),
        in_specs=[pl.BlockSpec(memory_space=pltpu.VMEM)] * 8,
        out_specs=pl.BlockSpec(memory_space=pltpu.VMEM),
        scratch_shapes=scratch,
        compiler_params=pltpu.CompilerParams(
            collective_id=0, has_side_effects=True, vmem_limit_bytes=56 * 1024 * 1024
        ),
    )(tokens, starts, gain[None], w_query, w_key, w_value, w_out, cotangent)


def solution(mesh):
    return jax.shard_map(
        per_device,
        mesh=mesh,
        in_specs=(
            P("dp", "ctx", None),
            P("dp", "ctx"),
            P(),
            P("dp", None),
            P("dp", None),
            P("dp", None),
            P("dp", None),
            P("dp", "ctx", None),
        ),
        out_specs=P("dp", "ctx", None),
        check_vma=False,
    )
```

```python
import functools
import math

import jax
import jax.numpy as jnp
from jax import lax
from jax.experimental import pallas as pl
from jax.experimental.pallas import tpu as pltpu
from jax.sharding import PartitionSpec as P

HEAD = 128
BF = jnp.bfloat16
F32 = jnp.float32


def dot(left, right, dims):
    return lax.dot_general(left, right, ((dims[0], dims[1]), ((), ())), preferred_element_type=F32)


def mm(left, right):
    return dot(left, right, ((1,), (0,)))


def mm_nt(left, right):
    return dot(left, right, ((1,), (1,)))


def mm_tn(left, right):
    return dot(left, right, ((0,), (0,)))


def remote(src, dst, send, recv, **where):
    return pltpu.make_async_remote_copy(
        src_ref=src, dst_ref=dst, send_sem=send, recv_sem=recv,
        device_id=where, device_id_type=pl.DeviceIdType.MESH,
    )


def kernel(
    n, dp,
    tok_hbm, starts, gain, wq, wk, wv, wo, cot_hbm, window, member,
    tok, cot, st_mine, st_near, near_out, near_in, head_out, head_in, gath, wcat, wout, grads, datt,
    qkv, dqkv, dkv, part, sib, red, rs, seg_out, seg_in,
    in_sem, st_send, st_recv, near_send, near_recv, head_send, head_recv, seg_send, seg_recv,
    w_send, w_recv, w_local, wo_send, wo_recv, wo_local, wo_fsend, wo_frecv,
    right_send, left_send, pair_send, gath_recv, datt_send, datt_recv,
    sib_send, sib_recv, rs_send, rs_recv,
):
    me = lax.axis_index("dp")
    c = lax.axis_index("ctx")
    core = lax.rem(c, 2)
    chip = lax.div(c, 2)
    chips = n // 2
    mate = c + 1 - 2 * core
    rows, width = tok.shape
    seg_dev = starts.shape[1]
    segs = n * seg_dev
    w_rows, inner = wq.shape
    half = w_rows // 2
    heads = inner // HEAD
    parts = n // heads
    h = lax.rem(c, heads)
    r = lax.div(c, heads)
    scale = 1.0 / math.sqrt(HEAD)
    has_prev, has_next = c > 0, c < n - 1

    barrier = pltpu.get_barrier_semaphore()
    for o in range(1, n):
        pl.semaphore_signal(barrier, inc=1, device_id={"ctx": lax.rem(c + o, n)},
                            device_id_type=pl.DeviceIdType.MESH)
    for o in range(1, dp):
        pl.semaphore_signal(barrier, inc=1, device_id={"dp": lax.rem(me + o, dp)},
                            device_id_type=pl.DeviceIdType.MESH)

    def dp_rows(where, extra=0, size=w_rows):
        return pl.ds(pl.multiple_of(where * w_rows + extra, size), size)

    cot_load = pltpu.make_async_copy(cot_hbm.at[0], cot, in_sem.at[0])
    tok_load = pltpu.make_async_copy(tok_hbm.at[0], tok, in_sem.at[1])
    head_at = pl.ds(pl.multiple_of(h * HEAD, HEAD), HEAD)
    mats = (wq, wk, wv)
    own_loads = [
        pltpu.make_async_copy(mats[i].at[:, head_at], wcat.at[dp_rows(me), pl.ds(i * HEAD, HEAD)],
                              w_local.at[i])
        for i in range(3)
    ]
    own_loads.append(pltpu.make_async_copy(wo, wout.at[dp_rows(me)], wo_local.at[0]))
    cot_load.start()
    tok_load.start()
    for load in own_loads:
        load.start()
    st_mine[...] = jnp.zeros_like(st_mine)
    st_mine[0:1, 0:seg_dev] = starts[...]
    pl.semaphore_wait(barrier, n - 1 + dp - 1)

    def to_next(src, dst, send, recv):
        return remote(src, dst.at[0], send.at[0], recv.at[0], ctx=c + 1)

    def to_prev(src, dst, send, recv):
        return remote(src, dst.at[1], send.at[1], recv.at[1], ctx=c - 1)

    def near_start(src_next, src_prev, dst, send, recv):
        @pl.when(has_next)
        def _():
            to_next(src_next, dst, send, recv).start()

        @pl.when(has_prev)
        def _():
            to_prev(src_prev, dst, send, recv).start()

    def near_wait(src_next, src_prev, dst, send, recv):
        @pl.when(has_prev)
        def _():
            to_next(src_next, dst, send, recv).wait_recv()
            to_prev(src_prev, dst, send, recv).wait_send()

        @pl.when(has_next)
        def _():
            to_prev(src_prev, dst, send, recv).wait_recv()
            to_next(src_next, dst, send, recv).wait_send()

    def near_clear(dst):
        @pl.when(jnp.logical_not(has_prev))
        def _():
            dst[0] = jnp.zeros_like(dst[0])

        @pl.when(jnp.logical_not(has_next))
        def _():
            dst[1] = jnp.zeros_like(dst[1])

    near_start(st_mine, st_mine, st_near, st_send, st_recv)

    def wo_copy(o):
        return remote(wo.at[pl.ds(pl.multiple_of(core * half, half), half)],
                      wout.at[dp_rows(me, core * half, half)],
                      wo_send.at[o - 1], wo_recv.at[o - 1], dp=lax.rem(me + o, dp))

    def wo_arrival(o, which, sends, recvs):
        at = dp_rows(lax.rem(me + dp - o, dp), which * half, half)
        return remote(wout.at[at], wout.at[at], sends.at[o - 1], recvs.at[o - 1], ctx=mate)

    for o in range(1, dp):
        wo_copy(o).start()

    def w_copy(o, i):
        return remote(mats[i].at[:, head_at], wcat.at[dp_rows(me), pl.ds(i * HEAD, HEAD)],
                      w_send.at[o - 1, i], w_recv.at[o - 1, i], dp=lax.rem(me + o, dp))

    def w_arrival(o, i):
        src = lax.rem(me + dp - o, dp)
        return remote(mats[i].at[:, head_at], wcat.at[dp_rows(src), pl.ds(i * HEAD, HEAD)],
                      w_send.at[o - 1, i], w_recv.at[o - 1, i], dp=lax.rem(me + o, dp))

    near_wait(st_mine, st_mine, st_near, st_send, st_recv)
    own_row = starts[...].astype(F32)
    prev_row = jnp.where(has_prev, st_near[0, 0:1, 0:seg_dev].astype(F32), -1.0)
    next_row = jnp.where(has_next, st_near[1, 0:1, 0:seg_dev].astype(F32), float(rows * n))
    sub = lax.broadcasted_iota(jnp.int32, (seg_dev, seg_dev), 0)
    lane = lax.broadcasted_iota(jnp.int32, (seg_dev, seg_dev), 1)

    def column(mask, row):
        return jnp.sum(jnp.where(mask, row, 0.0), axis=1, keepdims=True)

    def follow(row, after):
        edge = (sub == seg_dev - 1) & (lane == 0)
        return column(lane == sub + 1, row) + column(edge, after)

    same = lane == sub
    pos = (lax.broadcasted_iota(jnp.int32, (1, rows), 1) + c * rows).astype(F32)
    own_col, own_end = column(same, own_row), follow(own_row, next_row)
    end_row = jnp.full((1, seg_dev), float(rows * n), F32)

    def belongs(first, last):
        return jnp.where((first <= pos) & (pos < last), 1.0, 0.0).astype(BF)

    member[0:seg_dev] = belongs(column(same, prev_row), follow(prev_row, own_row))
    member[seg_dev:2 * seg_dev] = belongs(own_col, own_end)
    member[2 * seg_dev:] = belongs(column(same, next_row), follow(next_row, end_row))

    def near_args(kind):
        return (near_out.at[kind, 0], near_out.at[kind, 1], near_in.at[kind],
                near_send.at[kind], near_recv.at[kind])

    for kind, load, rows_ref in ((0, cot_load, cot), (1, tok_load, tok)):
        load.wait()
        near_out[kind, 0] = mm(member[2 * seg_dev:], rows_ref[...]).astype(BF)
        near_out[kind, 1] = mm(member[0:seg_dev], rows_ref[...]).astype(BF)
        near_start(*near_args(kind))
    for o in range(1, dp):
        for i in range(3):
            w_copy(o, i).start()
    sum_cot = mm(member[seg_dev:2 * seg_dev], cot[...])
    sum_tok = mm(member[seg_dev:2 * seg_dev], tok[...])
    for kind in range(2):
        near_clear(near_in.at[kind])

    near_wait(*near_args(0))
    grad_sum = sum_cot + near_in[0, 0].astype(F32) + near_in[0, 1].astype(F32)
    head_out[...] = grad_sum[0:8]

    def head_copy():
        return remote(head_out, head_in, head_send.at[0], head_recv.at[0], ctx=c - 1)

    @pl.when(has_prev)
    def _():
        head_copy().start()

    near_wait(*near_args(1))
    count = own_end - own_col
    pooled = (sum_tok + near_in[1, 0].astype(F32) + near_in[1, 1].astype(F32)) / count
    rms = jnp.sqrt(jnp.mean(pooled * pooled, axis=-1, keepdims=True) + 1e-06)
    normed = pooled / rms

    def spot(where):
        return gath.at[pl.ds(pl.multiple_of(where * seg_dev, seg_dev), seg_dev)]

    def hop(src_chip, sems, **where):
        at = 2 * src_chip + core
        return remote(spot(at), spot(at), sems.at[src_chip], gath_recv.at[at], **where)

    def go_right(src):
        return hop(src, right_send, ctx=c + 2)

    def go_left(src):
        return hop(src, left_send, ctx=c - 2)

    def go_pair(src):
        return hop(src, pair_send, ctx=mate)

    def arrival(where):
        return remote(spot(where), spot(where), right_send.at[0], gath_recv.at[where], ctx=mate)

    not_last, not_first = chip < chips - 1, chip > 0
    own_at = pl.ds(pl.multiple_of(c * seg_dev, seg_dev), seg_dev)
    gath[own_at] = (normed * gain[...]).astype(BF)

    @pl.when(not_last)
    def _():
        go_right(chip).start()

    @pl.when(not_first)
    def _():
        go_left(chip).start()

    go_pair(chip).start()

    def relay(s):
        @pl.when(chip - s >= 0)
        def _():
            arrival(c - 2 * s).wait_recv()

            @pl.when(not_last)
            def _():
                go_right(chip - s).start()

            go_pair(chip - s).start()

        @pl.when(chip + s < chips)
        def _():
            arrival(c + 2 * s).wait_recv()

            @pl.when(not_first)
            def _():
                go_left(chip + s).start()

            go_pair(chip + s).start()

    def datt_copy(o):
        to = lax.rem(c + o, n)
        cols = pl.ds(pl.multiple_of(lax.rem(to, heads) * HEAD, HEAD), HEAD)
        return remote(grads.at[:, cols], datt.at[own_at], datt_send.at[o - 1], datt_recv.at[o - 1],
                      ctx=to)

    def datt_arrival(o):
        src = lax.rem(c + n - o, n)
        at = pl.ds(pl.multiple_of(src * seg_dev, seg_dev), seg_dev)
        return remote(grads.at[:, head_at], datt.at[at], datt_send.at[o - 1], datt_recv.at[o - 1],
                      ctx=mate)

    def forward_wo():
        for o in range(1, dp):
            wo_arrival(o, core, wo_send, wo_recv).wait_recv()
            wo_arrival(o, core, wo_fsend, wo_frecv).start()

    def own_datt():
        own_loads[3].wait()
        for o in range(1, dp):
            wo_arrival(o, 1 - core, wo_fsend, wo_frecv).wait_recv()
        grads[...] = mm_nt(grad_sum.astype(BF), wout[...]).astype(BF)
        for o in range(1, n):
            datt_copy(o).start()
        datt[own_at] = grads[:, head_at]

    for s in range(1, chips):
        relay(s)
        if s == 1:
            forward_wo()
        if s == min(2, chips - 1):
            own_datt()

    for o in range(1, dp):
        for i in range(3):
            w_arrival(o, i).wait_recv()
    for load in own_loads[:3]:
        load.wait()
    for other in range(chips):
        arrival(2 * other + 1 - core).wait_recv()

    step = 512 if segs % 512 == 0 else seg_dev

    def project(b, _):
        at = pl.ds(pl.multiple_of(b * step, step), step)
        qkv[at] = mm(gath[at], wcat[...]).astype(BF)
        return 0

    lax.fori_loop(0, segs // step, project, 0)
    for o in range(1, n):
        datt_arrival(o).wait_recv()
    shifted = pltpu.roll(datt[...].astype(F32), segs - 1, 0)
    last = lax.broadcasted_iota(jnp.int32, (segs, HEAD), 0) == segs - 1
    datt[...] = jnp.where(last, 0.0, shifted).astype(BF)

    dkv[...] = jnp.zeros_like(dkv)
    if parts > 1:
        dqkv[...] = jnp.zeros_like(dqkv)
    block = 2 * seg_dev

    def attend(q_at, first, klen):
        q = qkv[q_at, 0:HEAD]
        key = qkv[0:klen, HEAD:2 * HEAD]
        value = qkv[0:klen, 2 * HEAD:]
        grad = datt[q_at]
        score = mm_nt(q, key) * scale
        allowed = (lax.broadcasted_iota(jnp.int32, (block, klen), 1)
                   <= lax.broadcasted_iota(jnp.int32, (block, klen), 0) + first)
        score = jnp.where(allowed, score, -1e30)
        peak = jnp.max(score, axis=-1, keepdims=True)
        expo = jnp.where(allowed, jnp.exp(score - peak), 0.0)
        probs = expo / jnp.sum(expo, axis=-1, keepdims=True)
        probs_b = probs.astype(BF)
        attended = mm(probs_b, value).astype(BF).astype(F32)
        delta = jnp.sum(grad.astype(F32) * attended, axis=-1, keepdims=True)
        dscore = (probs * (mm_nt(grad, value) - delta)).astype(BF)
        dqkv[q_at, 0:HEAD] = (mm(dscore, key) * scale).astype(BF)
        dkv[0:klen, 0:HEAD] += mm_tn(dscore, q)
        dkv[0:klen, HEAD:] += mm_tn(probs_b, grad)

    if parts > 1:
        per = segs // parts // block

        def body(b, _):
            first = pl.multiple_of((r * per + b) * block, block)
            attend(pl.ds(first, block), first, segs)
            return 0

        lax.fori_loop(0, per, body, 0)

    def sib_copy(t):
        return remote(part.at[1 - core, t], sib.at[t], sib_send.at[t], sib_recv.at[t], ctx=mate)

    def rs_copy(t):
        return remote(red.at[t], rs.at[chip], rs_send.at[t], rs_recv.at[chip], ctx=2 * t + core)

    def rs_arrival(t):
        return remote(red.at[t], rs.at[t], rs_send.at[t], rs_recv.at[t], ctx=mate)

    def term(t):
        at = slice(t * block, (t + 1) * block)
        dqkv[at, HEAD:2 * HEAD] = (dkv[at, 0:HEAD] * scale).astype(BF)
        dqkv[at, 2 * HEAD:] = dkv[at, HEAD:].astype(BF)
        both = mm_nt(dqkv[at], wcat[...])
        part[0, t] = both[0:seg_dev].astype(BF)
        part[1, t] = both[seg_dev:].astype(BF)
        sib_copy(t).start()

    def push(t):
        sib_copy(t).wait_recv()
        red[t] = (part[core, t].astype(F32) + sib[t].astype(F32)).astype(BF)

        @pl.when(chip != t)
        def _():
            rs_copy(t).start()

    for t in reversed(range(chips)):
        if parts == 1:
            attend(slice(t * block, (t + 1) * block), t * block, (t + 1) * block)
        term(t)
        if t + 1 < chips:
            push(t + 1)
    push(0)

    for other in range(chips):
        @pl.when(not_last & (other <= chip))
        def _():
            go_right(other).wait_send()

        @pl.when(not_first & (other >= chip))
        def _():
            go_left(other).wait_send()

        go_pair(other).wait_send()
        sib_copy(other).wait_send()
    for o in range(1, dp):
        for i in range(3):
            w_copy(o, i).wait_send()
        wo_copy(o).wait_send()
        wo_arrival(o, core, wo_fsend, wo_frecv).wait_send()
    for o in range(1, n):
        datt_copy(o).wait_send()

    @pl.when(has_prev)
    def _():
        head_copy().wait_send()

    @pl.when(has_next)
    def _():
        head_copy().wait_recv()

    @pl.when(jnp.logical_not(has_next))
    def _():
        head_in[...] = jnp.zeros_like(head_in)

    near_clear(seg_in)
    rolled = pltpu.roll(grad_sum, seg_dev - 1, 0)
    ends = lax.broadcasted_iota(jnp.int32, (seg_dev, width), 0) == seg_dev - 1
    dout = jnp.where(ends, head_in[0:1], rolled)

    dnormin = red[chip].astype(F32)
    for o in range(1, chips):
        t = lax.rem(chip + o, chips)
        rs_arrival(t).wait_recv()
        dnormin = dnormin + rs[t].astype(F32)

    scaled = dnormin * gain[...]
    dpooled = dout + (scaled - normed * jnp.mean(scaled * normed, axis=-1, keepdims=True)) / rms
    seg_out[...] = (dpooled / count).astype(BF)
    near_start(seg_out, seg_out, seg_in, seg_send, seg_recv)
    window[seg_dev:2 * seg_dev] = seg_out[...]
    for t in range(chips):
        @pl.when(chip != t)
        def _():
            rs_copy(t).wait_send()
    near_wait(seg_out, seg_out, seg_in, seg_send, seg_recv)
    window[0:seg_dev] = seg_in[0]
    window[2 * seg_dev:] = seg_in[1]


def per_device(tokens, starts, gain, w_query, w_key, w_value, w_out, cotangent):
    n, dp = lax.axis_size("ctx"), lax.axis_size("dp")
    chips = n // 2
    rows, width = tokens.shape[1:]
    seg_dev = starts.shape[1]
    segs = n * seg_dev
    dma = pltpu.SemaphoreType.DMA
    vmem = pltpu.VMEM
    scratch = [
        vmem((rows, width), BF), vmem((rows, width), BF),
        vmem((8, 128), jnp.int32), vmem((2, 8, 128), jnp.int32),
        vmem((2, 2, seg_dev, width), BF), vmem((2, 2, seg_dev, width), BF),
        vmem((8, width), F32), vmem((8, width), F32),
        vmem((segs, width), BF),
        vmem((width, 3 * HEAD), BF),
        vmem((dp * w_out.shape[0], width), BF),
        vmem((seg_dev, dp * w_out.shape[0]), BF),
        vmem((segs, HEAD), BF),
        vmem((segs, 3 * HEAD), BF),
        vmem((segs, 3 * HEAD), BF),
        vmem((segs, 2 * HEAD), F32),
        vmem((2, chips, seg_dev, width), BF),
        vmem((chips, seg_dev, width), BF),
        vmem((chips, seg_dev, width), BF),
        vmem((chips, seg_dev, width), BF),
        vmem((seg_dev, width), BF),
        vmem((2, seg_dev, width), BF),
        dma((2,)), dma((2,)), dma((2,)), dma((2, 2)), dma((2, 2)), dma((1,)), dma((1,)), dma((2,)), dma((2,)),
        dma((dp - 1, 3)), dma((dp - 1, 3)), dma((3,)),
        dma((dp - 1,)), dma((dp - 1,)), dma((1,)), dma((dp - 1,)), dma((dp - 1,)),
        dma((chips,)), dma((chips,)), dma((chips,)), dma((n,)), dma((n - 1,)), dma((n - 1,)),
        dma((chips,)), dma((chips,)), dma((chips,)), dma((chips,)),
    ]
    here, there = pl.BlockSpec(memory_space=pltpu.VMEM), pl.BlockSpec(memory_space=pl.ANY)
    window, member = pl.pallas_call(
        functools.partial(kernel, n, dp),
        out_shape=(
            jax.ShapeDtypeStruct((3 * seg_dev, width), BF),
            jax.ShapeDtypeStruct((3 * seg_dev, rows), BF),
        ),
        in_specs=[there, here, here, there, there, there, there, there],
        out_specs=(here, here),
        scratch_shapes=scratch,
        compiler_params=pltpu.CompilerParams(
            collective_id=0, has_side_effects=True, vmem_limit_bytes=56 * 1024 * 1024
        ),
    )(tokens, starts, gain[None], w_query, w_key, w_value, w_out, cotangent)
    return (cotangent[0].astype(F32) + mm_tn(member, window)).astype(BF)[None]


def solution(mesh):
    return jax.shard_map(
        per_device,
        mesh=mesh,
        in_specs=(
            P("dp", "ctx", None),
            P("dp", "ctx"),
            P(),
            P("dp", None),
            P("dp", None),
            P("dp", None),
            P("dp", None),
            P("dp", "ctx", None),
        ),
        out_specs=P("dp", "ctx", None),
        check_vma=False,
    )
```

```python
import functools
import math

import jax
import jax.numpy as jnp
from jax import lax
from jax.experimental import pallas as pl
from jax.experimental.pallas import tpu as pltpu
from jax.sharding import PartitionSpec as P

HEAD = 128
BF = jnp.bfloat16
F32 = jnp.float32


def dot(left, right, dims):
    return lax.dot_general(left, right, ((dims[0], dims[1]), ((), ())), preferred_element_type=F32)


def mm(left, right):
    return dot(left, right, ((1,), (0,)))


def mm_nt(left, right):
    return dot(left, right, ((1,), (1,)))


def mm_tn(left, right):
    return dot(left, right, ((0,), (0,)))


def remote(src, dst, send, recv, **where):
    return pltpu.make_async_remote_copy(
        src_ref=src, dst_ref=dst, send_sem=send, recv_sem=recv,
        device_id=where, device_id_type=pl.DeviceIdType.MESH,
    )


def kernel(
    n, dp,
    tok_hbm, starts, gain, wq, wk, wv, wo, cot_hbm, window, spread_at,
    member, tok, cot, st_mine, st_near, near_out, near_in, head_out, head_in, gath, wcat, wout, grads, datt,
    qkv, dqkv, dkv, prob_s, dscore_s, part, sib, red, rs, seg_out, seg_in,
    in_sem, st_send, st_recv, near_send, near_recv, head_send, head_recv, seg_send, seg_recv,
    w_send, w_recv, w_local, wo_send, wo_recv, wo_local, wo_fsend, wo_frecv,
    right_send, left_send, pair_send, gath_recv, datt_send, datt_recv,
    sib_send, sib_recv, rs_send, rs_recv,
):
    me = lax.axis_index("dp")
    c = lax.axis_index("ctx")
    core = lax.rem(c, 2)
    chip = lax.div(c, 2)
    chips = n // 2
    mate = c + 1 - 2 * core
    rows, width = tok.shape
    seg_dev = starts.shape[1]
    segs = n * seg_dev
    w_rows, inner = wq.shape
    half = w_rows // 2
    heads = inner // HEAD
    parts = n // heads
    h = lax.rem(c, heads)
    r = lax.div(c, heads)
    scale = 1.0 / math.sqrt(HEAD)
    has_prev, has_next = c > 0, c < n - 1

    barrier = pltpu.get_barrier_semaphore()
    for o in range(1, n):
        pl.semaphore_signal(barrier, inc=1, device_id={"ctx": lax.rem(c + o, n)},
                            device_id_type=pl.DeviceIdType.MESH)
    for o in range(1, dp):
        pl.semaphore_signal(barrier, inc=1, device_id={"dp": lax.rem(me + o, dp)},
                            device_id_type=pl.DeviceIdType.MESH)

    def dp_rows(where, extra=0, size=w_rows):
        return pl.ds(pl.multiple_of(where * w_rows + extra, size), size)

    cot_load = pltpu.make_async_copy(cot_hbm.at[0], cot, in_sem.at[0])
    tok_load = pltpu.make_async_copy(tok_hbm.at[0], tok, in_sem.at[1])
    head_at = pl.ds(pl.multiple_of(h * HEAD, HEAD), HEAD)
    mats = (wq, wk, wv)
    own_loads = [
        pltpu.make_async_copy(mats[i].at[:, head_at], wcat.at[dp_rows(me), pl.ds(i * HEAD, HEAD)],
                              w_local.at[i])
        for i in range(3)
    ]
    own_loads.append(pltpu.make_async_copy(wo, wout.at[dp_rows(me)], wo_local.at[0]))
    cot_load.start()
    tok_load.start()
    for load in own_loads:
        load.start()
    st_mine[...] = jnp.zeros_like(st_mine)
    st_mine[0:1, 0:seg_dev] = starts[...]
    pl.semaphore_wait(barrier, n - 1 + dp - 1)

    def to_next(src, dst, send, recv):
        return remote(src, dst.at[0], send.at[0], recv.at[0], ctx=c + 1)

    def to_prev(src, dst, send, recv):
        return remote(src, dst.at[1], send.at[1], recv.at[1], ctx=c - 1)

    def near_start(src_next, src_prev, dst, send, recv):
        @pl.when(has_next)
        def _():
            to_next(src_next, dst, send, recv).start()

        @pl.when(has_prev)
        def _():
            to_prev(src_prev, dst, send, recv).start()

    def near_wait(src_next, src_prev, dst, send, recv):
        @pl.when(has_prev)
        def _():
            to_next(src_next, dst, send, recv).wait_recv()
            to_prev(src_prev, dst, send, recv).wait_send()

        @pl.when(has_next)
        def _():
            to_prev(src_prev, dst, send, recv).wait_recv()
            to_next(src_next, dst, send, recv).wait_send()

    def near_clear(dst):
        @pl.when(jnp.logical_not(has_prev))
        def _():
            dst[0] = jnp.zeros_like(dst[0])

        @pl.when(jnp.logical_not(has_next))
        def _():
            dst[1] = jnp.zeros_like(dst[1])

    near_start(st_mine, st_mine, st_near, st_send, st_recv)

    def wo_copy(o):
        return remote(wo.at[pl.ds(pl.multiple_of(core * half, half), half)],
                      wout.at[dp_rows(me, core * half, half)],
                      wo_send.at[o - 1], wo_recv.at[o - 1], dp=lax.rem(me + o, dp))

    def wo_arrival(o, which, sends, recvs):
        at = dp_rows(lax.rem(me + dp - o, dp), which * half, half)
        return remote(wout.at[at], wout.at[at], sends.at[o - 1], recvs.at[o - 1], ctx=mate)

    for o in range(1, dp):
        wo_copy(o).start()

    def w_copy(o, i):
        return remote(mats[i].at[:, head_at], wcat.at[dp_rows(me), pl.ds(i * HEAD, HEAD)],
                      w_send.at[o - 1, i], w_recv.at[o - 1, i], dp=lax.rem(me + o, dp))

    def w_arrival(o, i):
        src = lax.rem(me + dp - o, dp)
        return remote(mats[i].at[:, head_at], wcat.at[dp_rows(src), pl.ds(i * HEAD, HEAD)],
                      w_send.at[o - 1, i], w_recv.at[o - 1, i], dp=lax.rem(me + o, dp))

    near_wait(st_mine, st_mine, st_near, st_send, st_recv)
    own_row = starts[...].astype(F32)
    prev_row = jnp.where(has_prev, st_near[0, 0:1, 0:seg_dev].astype(F32), -1.0)
    next_row = jnp.where(has_next, st_near[1, 0:1, 0:seg_dev].astype(F32), float(rows * n))
    sub = lax.broadcasted_iota(jnp.int32, (seg_dev, seg_dev), 0)
    lane = lax.broadcasted_iota(jnp.int32, (seg_dev, seg_dev), 1)

    def column(mask, row):
        return jnp.sum(jnp.where(mask, row, 0.0), axis=1, keepdims=True)

    def follow(row, after):
        edge = (sub == seg_dev - 1) & (lane == 0)
        return column(lane == sub + 1, row) + column(edge, after)

    same = lane == sub
    pos = (lax.broadcasted_iota(jnp.int32, (1, rows), 1) + c * rows).astype(F32)
    own_col, own_end = column(same, own_row), follow(own_row, next_row)
    end_row = jnp.full((1, seg_dev), float(rows * n), F32)

    def belongs(first, last):
        return jnp.where((first <= pos) & (pos < last), 1.0, 0.0).astype(BF)

    member[0:seg_dev] = belongs(column(same, prev_row), follow(prev_row, own_row))
    member[seg_dev:2 * seg_dev] = belongs(own_col, own_end)
    member[2 * seg_dev:] = belongs(column(same, next_row), follow(next_row, end_row))

    def near_args(kind):
        return (near_out.at[kind, 0], near_out.at[kind, 1], near_in.at[kind],
                near_send.at[kind], near_recv.at[kind])

    for kind, load, rows_ref in ((0, cot_load, cot), (1, tok_load, tok)):
        load.wait()
        near_out[kind, 0] = mm(member[2 * seg_dev:], rows_ref[...]).astype(BF)
        near_out[kind, 1] = mm(member[0:seg_dev], rows_ref[...]).astype(BF)
        near_start(*near_args(kind))
    sum_cot = mm(member[seg_dev:2 * seg_dev], cot[...])
    sum_tok = mm(member[seg_dev:2 * seg_dev], tok[...])
    for kind in range(2):
        near_clear(near_in.at[kind])

    def across(col):
        return jnp.sum(jnp.where(same, col, 0.0), axis=0, keepdims=True)

    pos_col = (lax.broadcasted_iota(jnp.int32, (rows, 1), 0) + c * rows).astype(F32)
    for k, (first, last) in enumerate((
        (prev_row, across(follow(prev_row, own_row))),
        (own_row, across(own_end)),
        (next_row, across(follow(next_row, end_row))),
    )):
        inside = (first <= pos_col) & (pos_col < last)
        spread_at[:, k * seg_dev:(k + 1) * seg_dev] = jnp.where(inside, 1.0, 0.0).astype(BF)

    near_wait(*near_args(0))
    grad_sum = sum_cot + near_in[0, 0].astype(F32) + near_in[0, 1].astype(F32)
    head_out[...] = grad_sum[0:8]

    def head_copy():
        return remote(head_out, head_in, head_send.at[0], head_recv.at[0], ctx=c - 1)

    @pl.when(has_prev)
    def _():
        head_copy().start()

    near_wait(*near_args(1))
    count = own_end - own_col
    pooled = (sum_tok + near_in[1, 0].astype(F32) + near_in[1, 1].astype(F32)) / count
    rms = jnp.sqrt(jnp.mean(pooled * pooled, axis=-1, keepdims=True) + 1e-06)
    normed = pooled / rms

    def spot(where):
        return gath.at[pl.ds(pl.multiple_of(where * seg_dev, seg_dev), seg_dev)]

    def hop(src_chip, sems, **where):
        at = 2 * src_chip + core
        return remote(spot(at), spot(at), sems.at[src_chip], gath_recv.at[at], **where)

    def go_right(src):
        return hop(src, right_send, ctx=c + 2)

    def go_left(src):
        return hop(src, left_send, ctx=c - 2)

    def go_pair(src):
        return hop(src, pair_send, ctx=mate)

    def arrival(where):
        return remote(spot(where), spot(where), right_send.at[0], gath_recv.at[where], ctx=mate)

    not_last, not_first = chip < chips - 1, chip > 0
    own_at = pl.ds(pl.multiple_of(c * seg_dev, seg_dev), seg_dev)
    gath[own_at] = (normed * gain[...]).astype(BF)

    @pl.when(not_last)
    def _():
        go_right(chip).start()

    @pl.when(not_first)
    def _():
        go_left(chip).start()

    go_pair(chip).start()
    for o in range(1, dp):
        for i in range(3):
            w_copy(o, i).start()

    def relay(s):
        @pl.when(chip - s >= 0)
        def _():
            arrival(c - 2 * s).wait_recv()

            @pl.when(not_last)
            def _():
                go_right(chip - s).start()

            go_pair(chip - s).start()

        @pl.when(chip + s < chips)
        def _():
            arrival(c + 2 * s).wait_recv()

            @pl.when(not_first)
            def _():
                go_left(chip + s).start()

            go_pair(chip + s).start()

    def datt_copy(o):
        to = lax.rem(c + o, n)
        cols = pl.ds(pl.multiple_of(lax.rem(to, heads) * HEAD, HEAD), HEAD)
        return remote(grads.at[:, cols], datt.at[own_at], datt_send.at[o - 1], datt_recv.at[o - 1],
                      ctx=to)

    def datt_arrival(o):
        src = lax.rem(c + n - o, n)
        at = pl.ds(pl.multiple_of(src * seg_dev, seg_dev), seg_dev)
        return remote(grads.at[:, head_at], datt.at[at], datt_send.at[o - 1], datt_recv.at[o - 1],
                      ctx=mate)

    def forward_wo():
        for o in range(1, dp):
            wo_arrival(o, core, wo_send, wo_recv).wait_recv()
            wo_arrival(o, core, wo_fsend, wo_frecv).start()

    def own_datt():
        own_loads[3].wait()
        for o in range(1, dp):
            wo_arrival(o, 1 - core, wo_fsend, wo_frecv).wait_recv()
        grads[...] = mm_nt(grad_sum.astype(BF), wout[...]).astype(BF)
        for o in range(1, n):
            datt_copy(o).start()
        datt[own_at] = grads[:, head_at]

    for s in range(1, chips):
        relay(s)
        if s == 1:
            forward_wo()
        if s == min(2, chips - 1):
            own_datt()

    for o in range(1, dp):
        for i in range(3):
            w_arrival(o, i).wait_recv()
    for load in own_loads[:3]:
        load.wait()
    for other in range(chips):
        arrival(2 * other + 1 - core).wait_recv()

    step = 512 if segs % 512 == 0 else seg_dev

    def project(b, _):
        at = pl.ds(pl.multiple_of(b * step, step), step)
        qkv[at] = mm(gath[at], wcat[...]).astype(BF)
        return 0

    lax.fori_loop(0, segs // step, project, 0)
    for o in range(1, n):
        datt_arrival(o).wait_recv()
    shifted = pltpu.roll(datt[...].astype(F32), segs - 1, 0)
    last = lax.broadcasted_iota(jnp.int32, (segs, HEAD), 0) == segs - 1
    datt[...] = jnp.where(last, 0.0, shifted).astype(BF)

    if parts > 1:
        dkv[...] = jnp.zeros_like(dkv)
        dqkv[...] = jnp.zeros_like(dqkv)
    block = 2 * seg_dev

    def attend(q_at, first, klen):
        q = qkv[q_at, 0:HEAD]
        key = qkv[0:klen, HEAD:2 * HEAD]
        value = qkv[0:klen, 2 * HEAD:]
        grad = datt[q_at]
        score = mm_nt(q, key) * scale
        allowed = (lax.broadcasted_iota(jnp.int32, (block, klen), 1)
                   <= lax.broadcasted_iota(jnp.int32, (block, klen), 0) + first)
        score = jnp.where(allowed, score, -1e30)
        peak = jnp.max(score, axis=-1, keepdims=True)
        expo = jnp.where(allowed, jnp.exp(score - peak), 0.0)
        probs = expo / jnp.sum(expo, axis=-1, keepdims=True)
        probs_b = probs.astype(BF)
        attended = mm(probs_b, value).astype(BF).astype(F32)
        delta = jnp.sum(grad.astype(F32) * attended, axis=-1, keepdims=True)
        dscore = (probs * (mm_nt(grad, value) - delta)).astype(BF)
        dqkv[q_at, 0:HEAD] = (mm(dscore, key) * scale).astype(BF)
        return q, grad, probs_b, dscore

    if parts > 1:
        per = segs // parts // block

        def body(b, _):
            first = pl.multiple_of((r * per + b) * block, block)
            q, grad, probs_b, dscore = attend(pl.ds(first, block), first, segs)
            dkv[:, 0:HEAD] += mm_tn(dscore, q)
            dkv[:, HEAD:] += mm_tn(probs_b, grad)
            return 0

        lax.fori_loop(0, per, body, 0)
    else:
        for t in range(chips):
            at, upto = slice(t * block, (t + 1) * block), (t + 1) * block
            _, _, probs_b, dscore = attend(at, t * block, upto)
            prob_s[at, 0:upto] = probs_b
            dscore_s[at, 0:upto] = dscore

    def sib_copy(t):
        return remote(part.at[1 - core, t], sib.at[t], sib_send.at[t], sib_recv.at[t], ctx=mate)

    def rs_copy(t):
        return remote(red.at[t], rs.at[chip], rs_send.at[t], rs_recv.at[chip], ctx=2 * t + core)

    def rs_arrival(t):
        return remote(red.at[t], rs.at[t], rs_send.at[t], rs_recv.at[t], ctx=mate)

    def term(t):
        at = slice(t * block, (t + 1) * block)
        if parts > 1:
            dkey, dvalue = dkv[at, 0:HEAD], dkv[at, HEAD:]
        else:
            dkey = mm_tn(dscore_s[t * block:, at], qkv[t * block:, 0:HEAD])
            dvalue = mm_tn(prob_s[t * block:, at], datt[t * block:])
        dqkv[at, HEAD:2 * HEAD] = (dkey * scale).astype(BF)
        dqkv[at, 2 * HEAD:] = dvalue.astype(BF)
        both = mm_nt(dqkv[at], wcat[...])
        part[0, t] = both[0:seg_dev].astype(BF)
        part[1, t] = both[seg_dev:].astype(BF)
        sib_copy(t).start()

    def push(t):
        sib_copy(t).wait_recv()
        red[t] = (part[core, t].astype(F32) + sib[t].astype(F32)).astype(BF)

        @pl.when(chip != t)
        def _():
            rs_copy(t).start()

    order = [t // 2 if t % 2 == 0 else chips - 1 - t // 2 for t in range(chips)]
    for at, t in enumerate(order):
        term(t)
        if at > 0:
            push(order[at - 1])
    push(order[-1])

    for other in range(chips):
        @pl.when(not_last & (other <= chip))
        def _():
            go_right(other).wait_send()

        @pl.when(not_first & (other >= chip))
        def _():
            go_left(other).wait_send()

        go_pair(other).wait_send()
        sib_copy(other).wait_send()
    for o in range(1, dp):
        for i in range(3):
            w_copy(o, i).wait_send()
        wo_copy(o).wait_send()
        wo_arrival(o, core, wo_fsend, wo_frecv).wait_send()
    for o in range(1, n):
        datt_copy(o).wait_send()

    @pl.when(has_prev)
    def _():
        head_copy().wait_send()

    @pl.when(has_next)
    def _():
        head_copy().wait_recv()

    @pl.when(jnp.logical_not(has_next))
    def _():
        head_in[...] = jnp.zeros_like(head_in)

    near_clear(seg_in)
    rolled = pltpu.roll(grad_sum, seg_dev - 1, 0)
    ends = lax.broadcasted_iota(jnp.int32, (seg_dev, width), 0) == seg_dev - 1
    dout = jnp.where(ends, head_in[0:1], rolled)

    dnormin = red[chip].astype(F32)
    for o in range(1, chips):
        t = lax.rem(chip + o, chips)
        rs_arrival(t).wait_recv()
        dnormin = dnormin + rs[t].astype(F32)

    scaled = dnormin * gain[...]
    dpooled = dout + (scaled - normed * jnp.mean(scaled * normed, axis=-1, keepdims=True)) / rms
    seg_out[...] = (dpooled / count).astype(BF)
    near_start(seg_out, seg_out, seg_in, seg_send, seg_recv)
    window[seg_dev:2 * seg_dev] = seg_out[...]
    for t in range(chips):
        @pl.when(chip != t)
        def _():
            rs_copy(t).wait_send()
    near_wait(seg_out, seg_out, seg_in, seg_send, seg_recv)
    window[0:seg_dev] = seg_in[0]
    window[2 * seg_dev:] = seg_in[1]


def per_device(tokens, starts, gain, w_query, w_key, w_value, w_out, cotangent):
    n, dp = lax.axis_size("ctx"), lax.axis_size("dp")
    chips = n // 2
    rows, width = tokens.shape[1:]
    seg_dev = starts.shape[1]
    segs = n * seg_dev
    dma = pltpu.SemaphoreType.DMA
    vmem = pltpu.VMEM
    heads = w_query.shape[1] // HEAD
    whole = n == heads
    scratch = [
        vmem((3 * seg_dev, rows), BF),
        vmem((rows, width), BF), vmem((rows, width), BF),
        vmem((8, 128), jnp.int32), vmem((2, 8, 128), jnp.int32),
        vmem((2, 2, seg_dev, width), BF), vmem((2, 2, seg_dev, width), BF),
        vmem((8, width), F32), vmem((8, width), F32),
        vmem((segs, width), BF),
        vmem((width, 3 * HEAD), BF),
        vmem((dp * w_out.shape[0], width), BF),
        vmem((seg_dev, dp * w_out.shape[0]), BF),
        vmem((segs, HEAD), BF),
        vmem((segs, 3 * HEAD), BF),
        vmem((segs, 3 * HEAD), BF),
        vmem((8, 2 * HEAD) if whole else (segs, 2 * HEAD), F32),
        vmem((segs, segs) if whole else (16, HEAD), BF),
        vmem((segs, segs) if whole else (16, HEAD), BF),
        vmem((2, chips, seg_dev, width), BF),
        vmem((chips, seg_dev, width), BF),
        vmem((chips, seg_dev, width), BF),
        vmem((chips, seg_dev, width), BF),
        vmem((seg_dev, width), BF),
        vmem((2, seg_dev, width), BF),
        dma((2,)), dma((2,)), dma((2,)), dma((2, 2)), dma((2, 2)), dma((1,)), dma((1,)), dma((2,)), dma((2,)),
        dma((dp - 1, 3)), dma((dp - 1, 3)), dma((3,)),
        dma((dp - 1,)), dma((dp - 1,)), dma((1,)), dma((dp - 1,)), dma((dp - 1,)),
        dma((chips,)), dma((chips,)), dma((chips,)), dma((n,)), dma((n - 1,)), dma((n - 1,)),
        dma((chips,)), dma((chips,)), dma((chips,)), dma((chips,)),
    ]
    here, there = pl.BlockSpec(memory_space=pltpu.VMEM), pl.BlockSpec(memory_space=pl.ANY)
    window, spread_at = pl.pallas_call(
        functools.partial(kernel, n, dp),
        out_shape=(
            jax.ShapeDtypeStruct((3 * seg_dev, width), BF),
            jax.ShapeDtypeStruct((rows, 3 * seg_dev), BF),
        ),
        in_specs=[there, here, here, there, there, there, there, there],
        out_specs=(here, here),
        scratch_shapes=scratch,
        compiler_params=pltpu.CompilerParams(
            collective_id=0, has_side_effects=True, vmem_limit_bytes=56 * 1024 * 1024
        ),
    )(tokens, starts, gain[None], w_query, w_key, w_value, w_out, cotangent)
    return (cotangent[0].astype(F32) + mm(spread_at, window)).astype(BF)[None]


def solution(mesh):
    return jax.shard_map(
        per_device,
        mesh=mesh,
        in_specs=(
            P("dp", "ctx", None),
            P("dp", "ctx"),
            P(),
            P("dp", None),
            P("dp", None),
            P("dp", None),
            P("dp", None),
            P("dp", "ctx", None),
        ),
        out_specs=P("dp", "ctx", None),
        check_vma=False,
    )
```

```python
import functools
import math

import jax
import jax.numpy as jnp
from jax import lax
from jax.experimental import pallas as pl
from jax.experimental.pallas import tpu as pltpu
from jax.sharding import PartitionSpec as P

HEAD = 128
BF = jnp.bfloat16
F32 = jnp.float32


def dot(left, right, dims):
    return lax.dot_general(left, right, ((dims[0], dims[1]), ((), ())), preferred_element_type=F32)


def mm(left, right):
    return dot(left, right, ((1,), (0,)))


def mm_nt(left, right):
    return dot(left, right, ((1,), (1,)))


def mm_tn(left, right):
    return dot(left, right, ((0,), (0,)))


def remote(src, dst, send, recv, **where):
    return pltpu.make_async_remote_copy(
        src_ref=src, dst_ref=dst, send_sem=send, recv_sem=recv,
        device_id=where, device_id_type=pl.DeviceIdType.MESH,
    )


def kernel(
    n, dp,
    tok_hbm, starts, gain, wq, wk, wv, wo, cot_hbm, window, spread_at,
    member, tok, cot, st_mine, st_near, near_out, near_in, head_out, head_in, gath, wcat, wout, grads, datt,
    qkv, dqkv, dkv, prob_s, dscore_s, part, sib, red, rs, seg_out, seg_in,
    in_sem, st_send, st_recv, near_send, near_recv, head_send, head_recv, seg_send, seg_recv,
    w_send, w_recv, w_local, wo_send, wo_recv, wo_local, wo_fsend, wo_frecv,
    right_send, left_send, pair_send, gath_recv, datt_send, datt_recv,
    sib_send, sib_recv, rs_send, rs_recv,
):
    me = lax.axis_index("dp")
    c = lax.axis_index("ctx")
    core = lax.rem(c, 2)
    chip = lax.div(c, 2)
    chips = n // 2
    mate = c + 1 - 2 * core
    rows, width = tok.shape
    seg_dev = starts.shape[1]
    segs = n * seg_dev
    w_rows, inner = wq.shape
    half = w_rows // 2
    heads = inner // HEAD
    parts = n // heads
    h = lax.rem(c, heads)
    r = lax.div(c, heads)
    scale = 1.0 / math.sqrt(HEAD)
    has_prev, has_next = c > 0, c < n - 1

    barrier = pltpu.get_barrier_semaphore()
    for o in range(1, n):
        pl.semaphore_signal(barrier, inc=1, device_id={"ctx": lax.rem(c + o, n)},
                            device_id_type=pl.DeviceIdType.MESH)
    for o in range(1, dp):
        pl.semaphore_signal(barrier, inc=1, device_id={"dp": lax.rem(me + o, dp)},
                            device_id_type=pl.DeviceIdType.MESH)

    def dp_rows(where, extra=0, size=w_rows):
        return pl.ds(pl.multiple_of(where * w_rows + extra, size), size)

    cot_load = pltpu.make_async_copy(cot_hbm.at[0], cot, in_sem.at[0])
    tok_load = pltpu.make_async_copy(tok_hbm.at[0], tok, in_sem.at[1])
    head_at = pl.ds(pl.multiple_of(h * HEAD, HEAD), HEAD)
    mats = (wq, wk, wv)
    own_loads = [
        pltpu.make_async_copy(mats[i].at[:, head_at], wcat.at[dp_rows(me), pl.ds(i * HEAD, HEAD)],
                              w_local.at[i])
        for i in range(3)
    ]
    own_loads.append(pltpu.make_async_copy(wo, wout.at[dp_rows(me)], wo_local.at[0]))
    cot_load.start()
    tok_load.start()
    for load in own_loads:
        load.start()
    st_mine[...] = jnp.zeros_like(st_mine)
    st_mine[0:1, 0:seg_dev] = starts[...]
    pl.semaphore_wait(barrier, n - 1 + dp - 1)

    def to_next(src, dst, send, recv):
        return remote(src, dst.at[0], send.at[0], recv.at[0], ctx=c + 1)

    def to_prev(src, dst, send, recv):
        return remote(src, dst.at[1], send.at[1], recv.at[1], ctx=c - 1)

    def near_start(src_next, src_prev, dst, send, recv):
        @pl.when(has_next)
        def _():
            to_next(src_next, dst, send, recv).start()

        @pl.when(has_prev)
        def _():
            to_prev(src_prev, dst, send, recv).start()

    def near_wait(src_next, src_prev, dst, send, recv):
        @pl.when(has_prev)
        def _():
            to_next(src_next, dst, send, recv).wait_recv()
            to_prev(src_prev, dst, send, recv).wait_send()

        @pl.when(has_next)
        def _():
            to_prev(src_prev, dst, send, recv).wait_recv()
            to_next(src_next, dst, send, recv).wait_send()

    def near_clear(dst):
        @pl.when(jnp.logical_not(has_prev))
        def _():
            dst[0] = jnp.zeros_like(dst[0])

        @pl.when(jnp.logical_not(has_next))
        def _():
            dst[1] = jnp.zeros_like(dst[1])

    near_start(st_mine, st_mine, st_near, st_send, st_recv)

    def wo_copy(o):
        return remote(wo.at[pl.ds(pl.multiple_of(core * half, half), half)],
                      wout.at[dp_rows(me, core * half, half)],
                      wo_send.at[o - 1], wo_recv.at[o - 1], dp=lax.rem(me + o, dp))

    def wo_arrival(o, which, sends, recvs):
        at = dp_rows(lax.rem(me + dp - o, dp), which * half, half)
        return remote(wout.at[at], wout.at[at], sends.at[o - 1], recvs.at[o - 1], ctx=mate)

    for o in range(1, dp):
        wo_copy(o).start()

    def w_copy(o, i):
        return remote(mats[i].at[:, head_at], wcat.at[dp_rows(me), pl.ds(i * HEAD, HEAD)],
                      w_send.at[o - 1, i], w_recv.at[o - 1, i], dp=lax.rem(me + o, dp))

    def w_arrival(o, i):
        src = lax.rem(me + dp - o, dp)
        return remote(mats[i].at[:, head_at], wcat.at[dp_rows(src), pl.ds(i * HEAD, HEAD)],
                      w_send.at[o - 1, i], w_recv.at[o - 1, i], dp=lax.rem(me + o, dp))

    near_wait(st_mine, st_mine, st_near, st_send, st_recv)
    own_row = starts[...].astype(F32)
    prev_row = jnp.where(has_prev, st_near[0, 0:1, 0:seg_dev].astype(F32), -1.0)
    next_row = jnp.where(has_next, st_near[1, 0:1, 0:seg_dev].astype(F32), float(rows * n))
    sub = lax.broadcasted_iota(jnp.int32, (seg_dev, seg_dev), 0)
    lane = lax.broadcasted_iota(jnp.int32, (seg_dev, seg_dev), 1)

    def column(mask, row):
        return jnp.sum(jnp.where(mask, row, 0.0), axis=1, keepdims=True)

    def follow(row, after):
        edge = (sub == seg_dev - 1) & (lane == 0)
        return column(lane == sub + 1, row) + column(edge, after)

    same = lane == sub
    pos = (lax.broadcasted_iota(jnp.int32, (1, rows), 1) + c * rows).astype(F32)
    own_col, own_end = column(same, own_row), follow(own_row, next_row)
    end_row = jnp.full((1, seg_dev), float(rows * n), F32)

    def belongs(first, last):
        return jnp.where((first <= pos) & (pos < last), 1.0, 0.0).astype(BF)

    member[0:seg_dev] = belongs(column(same, prev_row), follow(prev_row, own_row))
    member[seg_dev:2 * seg_dev] = belongs(own_col, own_end)
    member[2 * seg_dev:] = belongs(column(same, next_row), follow(next_row, end_row))

    def near_args(kind):
        return (near_out.at[kind, 0], near_out.at[kind, 1], near_in.at[kind],
                near_send.at[kind], near_recv.at[kind])

    for kind, load, rows_ref in ((0, cot_load, cot), (1, tok_load, tok)):
        load.wait()
        near_out[kind, 0] = mm(member[2 * seg_dev:], rows_ref[...]).astype(BF)
        near_out[kind, 1] = mm(member[0:seg_dev], rows_ref[...]).astype(BF)
        near_start(*near_args(kind))
    sum_cot = mm(member[seg_dev:2 * seg_dev], cot[...])
    sum_tok = mm(member[seg_dev:2 * seg_dev], tok[...])
    for kind in range(2):
        near_clear(near_in.at[kind])

    def across(col):
        return jnp.sum(jnp.where(same, col, 0.0), axis=0, keepdims=True)

    pos_col = (lax.broadcasted_iota(jnp.int32, (rows, 1), 0) + c * rows).astype(F32)
    for k, (first, last) in enumerate((
        (prev_row, across(follow(prev_row, own_row))),
        (own_row, across(own_end)),
        (next_row, across(follow(next_row, end_row))),
    )):
        inside = (first <= pos_col) & (pos_col < last)
        spread_at[:, k * seg_dev:(k + 1) * seg_dev] = jnp.where(inside, 1.0, 0.0).astype(BF)

    near_wait(*near_args(0))
    grad_sum = sum_cot + near_in[0, 0].astype(F32) + near_in[0, 1].astype(F32)
    head_out[...] = grad_sum[0:8]

    def head_copy():
        return remote(head_out, head_in, head_send.at[0], head_recv.at[0], ctx=c - 1)

    @pl.when(has_prev)
    def _():
        head_copy().start()

    near_wait(*near_args(1))
    count = own_end - own_col
    pooled = (sum_tok + near_in[1, 0].astype(F32) + near_in[1, 1].astype(F32)) / count
    rms = jnp.sqrt(jnp.mean(pooled * pooled, axis=-1, keepdims=True) + 1e-06)
    normed = pooled / rms

    def spot(where):
        return gath.at[pl.ds(pl.multiple_of(where * seg_dev, seg_dev), seg_dev)]

    def hop(src_chip, sems, **where):
        at = 2 * src_chip + core
        return remote(spot(at), spot(at), sems.at[src_chip], gath_recv.at[at], **where)

    def go_right(src):
        return hop(src, right_send, ctx=c + 2)

    def go_left(src):
        return hop(src, left_send, ctx=c - 2)

    def go_pair(src):
        return hop(src, pair_send, ctx=mate)

    def arrival(where):
        return remote(spot(where), spot(where), right_send.at[0], gath_recv.at[where], ctx=mate)

    not_last, not_first = chip < chips - 1, chip > 0
    own_at = pl.ds(pl.multiple_of(c * seg_dev, seg_dev), seg_dev)
    gath[own_at] = (normed * gain[...]).astype(BF)

    @pl.when(not_last)
    def _():
        go_right(chip).start()

    @pl.when(not_first)
    def _():
        go_left(chip).start()

    go_pair(chip).start()
    for o in range(1, dp):
        for i in range(3):
            w_copy(o, i).start()

    def relay(s):
        @pl.when(chip - s >= 0)
        def _():
            arrival(c - 2 * s).wait_recv()

            @pl.when(not_last)
            def _():
                go_right(chip - s).start()

            go_pair(chip - s).start()

        @pl.when(chip + s < chips)
        def _():
            arrival(c + 2 * s).wait_recv()

            @pl.when(not_first)
            def _():
                go_left(chip + s).start()

            go_pair(chip + s).start()

    def datt_copy(o):
        to = lax.rem(c + o, n)
        cols = pl.ds(pl.multiple_of(lax.rem(to, heads) * HEAD, HEAD), HEAD)
        return remote(grads.at[:, cols], datt.at[own_at], datt_send.at[o - 1], datt_recv.at[o - 1],
                      ctx=to)

    def datt_arrival(o):
        src = lax.rem(c + n - o, n)
        at = pl.ds(pl.multiple_of(src * seg_dev, seg_dev), seg_dev)
        return remote(grads.at[:, head_at], datt.at[at], datt_send.at[o - 1], datt_recv.at[o - 1],
                      ctx=mate)

    def forward_wo():
        for o in range(1, dp):
            wo_arrival(o, core, wo_send, wo_recv).wait_recv()
            wo_arrival(o, core, wo_fsend, wo_frecv).start()

    def own_datt():
        own_loads[3].wait()
        for o in range(1, dp):
            wo_arrival(o, 1 - core, wo_fsend, wo_frecv).wait_recv()
        grads[...] = mm_nt(grad_sum.astype(BF), wout[...]).astype(BF)
        for o in range(1, n):
            datt_copy(o).start()
        datt[own_at] = grads[:, head_at]

    for s in range(1, chips):
        relay(s)
        if s == 1:
            forward_wo()
        if s == min(2, chips - 1):
            own_datt()

    for o in range(1, dp):
        for i in range(3):
            w_arrival(o, i).wait_recv()
    for load in own_loads[:3]:
        load.wait()
    for other in range(chips):
        arrival(2 * other + 1 - core).wait_recv()

    step = 512 if segs % 512 == 0 else seg_dev

    def project(b, _):
        at = pl.ds(pl.multiple_of(b * step, step), step)
        qkv[at] = mm(gath[at], wcat[...]).astype(BF)
        return 0

    lax.fori_loop(0, segs // step, project, 0)
    for o in range(1, n):
        datt_arrival(o).wait_recv()
    shifted = pltpu.roll(datt[...].astype(F32), segs - 1, 0)
    last = lax.broadcasted_iota(jnp.int32, (segs, HEAD), 0) == segs - 1
    datt[...] = jnp.where(last, 0.0, shifted).astype(BF)

    if parts > 1:
        dkv[...] = jnp.zeros_like(dkv)
        dqkv[...] = jnp.zeros_like(dqkv)
    block = 2 * seg_dev

    def attend(q_at, first, klen):
        q = qkv[q_at, 0:HEAD]
        key = qkv[0:klen, HEAD:2 * HEAD]
        value = qkv[0:klen, 2 * HEAD:]
        grad = datt[q_at]
        score = mm_nt(q, key) * scale
        allowed = (lax.broadcasted_iota(jnp.int32, (block, klen), 1)
                   <= lax.broadcasted_iota(jnp.int32, (block, klen), 0) + first)
        score = jnp.where(allowed, score, -1e30)
        peak = jnp.max(score, axis=-1, keepdims=True)
        expo = jnp.where(allowed, jnp.exp(score - peak), 0.0)
        probs = expo / jnp.sum(expo, axis=-1, keepdims=True)
        probs_b = probs.astype(BF)
        attended = mm(probs_b, value).astype(BF).astype(F32)
        delta = jnp.sum(grad.astype(F32) * attended, axis=-1, keepdims=True)
        dscore = (probs * (mm_nt(grad, value) - delta)).astype(BF)
        dqkv[q_at, 0:HEAD] = (mm(dscore, key) * scale).astype(BF)
        return q, grad, probs_b, dscore

    if parts > 1:
        per = segs // parts // block

        def body(b, _):
            first = pl.multiple_of((r * per + b) * block, block)
            q, grad, probs_b, dscore = attend(pl.ds(first, block), first, segs)
            dkv[:, 0:HEAD] += mm_tn(dscore, q)
            dkv[:, HEAD:] += mm_tn(probs_b, grad)
            return 0

        lax.fori_loop(0, per, body, 0)
    else:
        for t in range(chips):
            at, upto = slice(t * block, (t + 1) * block), (t + 1) * block
            _, _, probs_b, dscore = attend(at, t * block, upto)
            prob_s[at, 0:upto] = probs_b
            dscore_s[at, 0:upto] = dscore

    def sib_copy(t):
        return remote(part.at[1 - core, t], sib.at[t], sib_send.at[t], sib_recv.at[t], ctx=mate)

    def piece(k):
        return pl.ds(k * (seg_dev // 2), seg_dev // 2)

    def way(leftward):
        side = jnp.where(leftward, 0, 1)
        return side, c + 4 * side - 2

    def rs_copy(t, k, leftward):
        side, to = way(leftward)
        return remote(red.at[t, piece(k)], rs.at[side, t, piece(k)],
                      rs_send.at[t, k], rs_recv.at[side, t, k], ctx=to)

    def rs_arrival(t, k, side):
        return remote(red.at[t, piece(k)], rs.at[side, t, piece(k)],
                      rs_send.at[t, k], rs_recv.at[side, t, k], ctx=mate)

    def term(t):
        at = slice(t * block, (t + 1) * block)
        if parts > 1:
            dkey, dvalue = dkv[at, 0:HEAD], dkv[at, HEAD:]
        else:
            dkey = mm_tn(dscore_s[t * block:, at], qkv[t * block:, 0:HEAD])
            dvalue = mm_tn(prob_s[t * block:, at], datt[t * block:])
        dqkv[at, HEAD:2 * HEAD] = (dkey * scale).astype(BF)
        dqkv[at, 2 * HEAD:] = dvalue.astype(BF)
        both = mm_nt(dqkv[at], wcat[...])
        part[0, t] = both[0:seg_dev].astype(BF)
        part[1, t] = both[seg_dev:].astype(BF)
        sib_copy(t).start()

    def push(t):
        sib_copy(t).wait_recv()
        red[t] = (part[core, t].astype(F32) + sib[t].astype(F32)).astype(BF)

        if t > 0:
            @pl.when(chip == 0)
            def _():
                for k in range(2):
                    rs_copy(t, k, False).start()
        if t < chips - 1:
            @pl.when(chip == chips - 1)
            def _():
                for k in range(2):
                    rs_copy(t, k, True).start()

    order = [t // 2 if t % 2 == 0 else chips - 1 - t // 2 for t in range(chips)]
    for at, t in enumerate(order):
        term(t)
        if at > 0:
            push(order[at - 1])
    push(order[-1])

    def pass_on(i, leftward):
        t = jnp.where(leftward, i, chips - 1 - i)
        inner_chip = (chip > 0) & (chip < chips - 1)
        passes = jnp.where(leftward, chip - t, t - chip) > 0

        @pl.when(inner_chip & passes)
        def _():
            side, _ = way(leftward)
            for k in range(2):
                rs_arrival(t, k, side).wait_recv()
                at = piece(k)
                red[t, at] = (red[t, at].astype(F32) + rs[side, t, at].astype(F32)).astype(BF)
                rs_copy(t, k, leftward).start()

    left_first = 2 * chip >= chips
    for i in range(chips - 1):
        pass_on(i, left_first)
        pass_on(i, jnp.logical_not(left_first))

    for other in range(chips):
        @pl.when(not_last & (other <= chip))
        def _():
            go_right(other).wait_send()

        @pl.when(not_first & (other >= chip))
        def _():
            go_left(other).wait_send()

        go_pair(other).wait_send()
        sib_copy(other).wait_send()
    for o in range(1, dp):
        for i in range(3):
            w_copy(o, i).wait_send()
        wo_copy(o).wait_send()
        wo_arrival(o, core, wo_fsend, wo_frecv).wait_send()
    for o in range(1, n):
        datt_copy(o).wait_send()

    @pl.when(has_prev)
    def _():
        head_copy().wait_send()

    @pl.when(has_next)
    def _():
        head_copy().wait_recv()

    @pl.when(jnp.logical_not(has_next))
    def _():
        head_in[...] = jnp.zeros_like(head_in)

    near_clear(seg_in)
    rolled = pltpu.roll(grad_sum, seg_dev - 1, 0)
    ends = lax.broadcasted_iota(jnp.int32, (seg_dev, width), 0) == seg_dev - 1
    dout = jnp.where(ends, head_in[0:1], rolled)

    @pl.when(chip == chips - 1)
    def _():
        rs[0, chips - 1] = jnp.zeros_like(rs[0, chips - 1])

    @pl.when(chip == 0)
    def _():
        rs[1, 0] = jnp.zeros_like(rs[1, 0])

    for k in range(2):
        @pl.when(not_first)
        def _():
            rs_arrival(chip, k, 1).wait_recv()

        @pl.when(not_last)
        def _():
            rs_arrival(chip, k, 0).wait_recv()

    dnormin = red[chip].astype(F32) + rs[0, chip].astype(F32) + rs[1, chip].astype(F32)

    scaled = dnormin * gain[...]
    dpooled = dout + (scaled - normed * jnp.mean(scaled * normed, axis=-1, keepdims=True)) / rms
    seg_out[...] = (dpooled / count).astype(BF)
    near_start(seg_out, seg_out, seg_in, seg_send, seg_recv)
    window[seg_dev:2 * seg_dev] = seg_out[...]
    for t in range(chips):
        @pl.when(chip != t)
        def _():
            for k in range(2):
                rs_arrival(t, k, 0).wait_send()
    near_wait(seg_out, seg_out, seg_in, seg_send, seg_recv)
    window[0:seg_dev] = seg_in[0]
    window[2 * seg_dev:] = seg_in[1]


def spread_kernel(spread_at, window, cot, out):
    out[0] = (cot[0].astype(F32) + mm(spread_at[...], window[...])).astype(BF)


def per_device(tokens, starts, gain, w_query, w_key, w_value, w_out, cotangent):
    n, dp = lax.axis_size("ctx"), lax.axis_size("dp")
    chips = n // 2
    rows, width = tokens.shape[1:]
    seg_dev = starts.shape[1]
    segs = n * seg_dev
    dma = pltpu.SemaphoreType.DMA
    vmem = pltpu.VMEM
    heads = w_query.shape[1] // HEAD
    whole = n == heads
    scratch = [
        vmem((3 * seg_dev, rows), BF),
        vmem((rows, width), BF), vmem((rows, width), BF),
        vmem((8, 128), jnp.int32), vmem((2, 8, 128), jnp.int32),
        vmem((2, 2, seg_dev, width), BF), vmem((2, 2, seg_dev, width), BF),
        vmem((8, width), F32), vmem((8, width), F32),
        vmem((segs, width), BF),
        vmem((width, 3 * HEAD), BF),
        vmem((dp * w_out.shape[0], width), BF),
        vmem((seg_dev, dp * w_out.shape[0]), BF),
        vmem((segs, HEAD), BF),
        vmem((segs, 3 * HEAD), BF),
        vmem((segs, 3 * HEAD), BF),
        vmem((8, 2 * HEAD) if whole else (segs, 2 * HEAD), F32),
        vmem((segs, segs) if whole else (16, HEAD), BF),
        vmem((segs, segs) if whole else (16, HEAD), BF),
        vmem((2, chips, seg_dev, width), BF),
        vmem((chips, seg_dev, width), BF),
        vmem((chips, seg_dev, width), BF),
        vmem((2, chips, seg_dev, width), BF),
        vmem((seg_dev, width), BF),
        vmem((2, seg_dev, width), BF),
        dma((2,)), dma((2,)), dma((2,)), dma((2, 2)), dma((2, 2)), dma((1,)), dma((1,)), dma((2,)), dma((2,)),
        dma((dp - 1, 3)), dma((dp - 1, 3)), dma((3,)),
        dma((dp - 1,)), dma((dp - 1,)), dma((1,)), dma((dp - 1,)), dma((dp - 1,)),
        dma((chips,)), dma((chips,)), dma((chips,)), dma((n,)), dma((n - 1,)), dma((n - 1,)),
        dma((chips,)), dma((chips,)), dma((chips, 2)), dma((2, chips, 2)),
    ]
    here, there = pl.BlockSpec(memory_space=pltpu.VMEM), pl.BlockSpec(memory_space=pl.ANY)
    window, spread_at = pl.pallas_call(
        functools.partial(kernel, n, dp),
        out_shape=(
            jax.ShapeDtypeStruct((3 * seg_dev, width), BF),
            jax.ShapeDtypeStruct((rows, 3 * seg_dev), BF),
        ),
        in_specs=[there, here, here, there, there, there, there, there],
        out_specs=(here, here),
        scratch_shapes=scratch,
        compiler_params=pltpu.CompilerParams(
            collective_id=0, has_side_effects=True, vmem_limit_bytes=56 * 1024 * 1024
        ),
    )(tokens, starts, gain[None], w_query, w_key, w_value, w_out, cotangent)
    step = 128
    return pl.pallas_call(
        spread_kernel,
        grid=(rows // step,),
        out_shape=jax.ShapeDtypeStruct(tokens.shape, BF),
        in_specs=[
            pl.BlockSpec((step, 3 * seg_dev), lambda i: (i, 0)),
            pl.BlockSpec((3 * seg_dev, width), lambda i: (0, 0)),
            pl.BlockSpec((1, step, width), lambda i: (0, i, 0)),
        ],
        out_specs=pl.BlockSpec((1, step, width), lambda i: (0, i, 0)),
        compiler_params=pltpu.CompilerParams(vmem_limit_bytes=16 * 1024 * 1024),
    )(spread_at, window, cotangent)


def solution(mesh):
    return jax.shard_map(
        per_device,
        mesh=mesh,
        in_specs=(
            P("dp", "ctx", None),
            P("dp", "ctx"),
            P(),
            P("dp", None),
            P("dp", None),
            P("dp", None),
            P("dp", None),
            P("dp", "ctx", None),
        ),
        out_specs=P("dp", "ctx", None),
        check_vma=False,
    )
```

```python
import functools
import math

import jax
import jax.numpy as jnp
from jax import lax
from jax.experimental import pallas as pl
from jax.experimental.pallas import tpu as pltpu
from jax.sharding import PartitionSpec as P

HEAD = 128
BF = jnp.bfloat16
F32 = jnp.float32


def dot(left, right, dims):
    return lax.dot_general(left, right, ((dims[0], dims[1]), ((), ())), preferred_element_type=F32)


def mm(left, right):
    return dot(left, right, ((1,), (0,)))


def mm_nt(left, right):
    return dot(left, right, ((1,), (1,)))


def mm_tn(left, right):
    return dot(left, right, ((0,), (0,)))


def remote(src, dst, send, recv, **where):
    return pltpu.make_async_remote_copy(
        src_ref=src, dst_ref=dst, send_sem=send, recv_sem=recv,
        device_id=where, device_id_type=pl.DeviceIdType.MESH,
    )


def kernel(
    n, dp,
    tok_hbm, starts, gain, wq, wk, wv, wo, cot_hbm, window, member,
    tok, cot, st_mine, st_near, near_out, near_in, head_out, head_in, gath, wcat, gsum, grads, datt,
    qkv, dqkv, dkv, part, sib, red, rs, seg_out, seg_in,
    in_sem, st_send, st_recv, near_send, near_recv, head_send, head_recv, seg_send, seg_recv,
    w_send, w_recv, w_local, g_send, g_recv,
    right_send, left_send, pair_send, gath_recv, datt_send, datt_recv,
    sib_send, sib_recv, rs_send, rs_recv,
):
    me = lax.axis_index("dp")
    c = lax.axis_index("ctx")
    core = lax.rem(c, 2)
    chip = lax.div(c, 2)
    chips = n // 2
    mate = c + 1 - 2 * core
    rows, width = tok.shape
    seg_dev = starts.shape[1]
    segs = n * seg_dev
    w_rows, inner = wq.shape
    heads = inner // HEAD
    parts = n // heads
    h = lax.rem(c, heads)
    r = lax.div(c, heads)
    scale = 1.0 / math.sqrt(HEAD)
    has_prev, has_next = c > 0, c < n - 1

    barrier = pltpu.get_barrier_semaphore()
    for o in range(1, n):
        pl.semaphore_signal(barrier, inc=1, device_id={"ctx": lax.rem(c + o, n)},
                            device_id_type=pl.DeviceIdType.MESH)
    for o in range(1, dp):
        pl.semaphore_signal(barrier, inc=1, device_id={"dp": lax.rem(me + o, dp)},
                            device_id_type=pl.DeviceIdType.MESH)
    per_row = w_rows // HEAD
    holder = lax.div(h, per_row)
    lone = jnp.where(holder == me, 1, 0)
    for o in range(n):
        @pl.when((holder != me) | (c != o))
        def _():
            pl.semaphore_signal(barrier, inc=1, device_id={"dp": holder, "ctx": o},
                                device_id_type=pl.DeviceIdType.MESH)

    def dp_rows(where, extra=0, size=w_rows):
        return pl.ds(pl.multiple_of(where * w_rows + extra, size), size)

    cot_load = pltpu.make_async_copy(cot_hbm.at[0], cot, in_sem.at[0])
    tok_load = pltpu.make_async_copy(tok_hbm.at[0], tok, in_sem.at[1])
    head_at = pl.ds(pl.multiple_of(h * HEAD, HEAD), HEAD)
    mats = (wq, wk, wv)
    own_loads = [
        pltpu.make_async_copy(mats[i].at[:, head_at], wcat.at[dp_rows(me), pl.ds(i * HEAD, HEAD)],
                              w_local.at[i])
        for i in range(3)
    ]
    cot_load.start()
    tok_load.start()
    for load in own_loads:
        load.start()
    st_mine[...] = jnp.zeros_like(st_mine)
    st_mine[0:1, 0:seg_dev] = starts[...]
    pl.semaphore_wait(barrier, n - 1 + dp - 1 + n - lone)

    def to_next(src, dst, send, recv):
        return remote(src, dst.at[0], send.at[0], recv.at[0], ctx=c + 1)

    def to_prev(src, dst, send, recv):
        return remote(src, dst.at[1], send.at[1], recv.at[1], ctx=c - 1)

    def near_start(src_next, src_prev, dst, send, recv):
        @pl.when(has_next)
        def _():
            to_next(src_next, dst, send, recv).start()

        @pl.when(has_prev)
        def _():
            to_prev(src_prev, dst, send, recv).start()

    def near_wait(src_next, src_prev, dst, send, recv):
        @pl.when(has_prev)
        def _():
            to_next(src_next, dst, send, recv).wait_recv()
            to_prev(src_prev, dst, send, recv).wait_send()

        @pl.when(has_next)
        def _():
            to_prev(src_prev, dst, send, recv).wait_recv()
            to_next(src_next, dst, send, recv).wait_send()

    def near_clear(dst):
        @pl.when(jnp.logical_not(has_prev))
        def _():
            dst[0] = jnp.zeros_like(dst[0])

        @pl.when(jnp.logical_not(has_next))
        def _():
            dst[1] = jnp.zeros_like(dst[1])

    near_start(st_mine, st_mine, st_near, st_send, st_recv)

    def w_copy(o, i):
        return remote(mats[i].at[:, head_at], wcat.at[dp_rows(me), pl.ds(i * HEAD, HEAD)],
                      w_send.at[o - 1, i], w_recv.at[o - 1, i], dp=lax.rem(me + o, dp))

    def w_arrival(o, i):
        src = lax.rem(me + dp - o, dp)
        return remote(mats[i].at[:, head_at], wcat.at[dp_rows(src), pl.ds(i * HEAD, HEAD)],
                      w_send.at[o - 1, i], w_recv.at[o - 1, i], dp=lax.rem(me + o, dp))

    for o in range(1, dp):
        for i in range(3):
            w_copy(o, i).start()

    near_wait(st_mine, st_mine, st_near, st_send, st_recv)
    own_row = starts[...].astype(F32)
    prev_row = jnp.where(has_prev, st_near[0, 0:1, 0:seg_dev].astype(F32), -1.0)
    next_row = jnp.where(has_next, st_near[1, 0:1, 0:seg_dev].astype(F32), float(rows * n))
    sub = lax.broadcasted_iota(jnp.int32, (seg_dev, seg_dev), 0)
    lane = lax.broadcasted_iota(jnp.int32, (seg_dev, seg_dev), 1)

    def column(mask, row):
        return jnp.sum(jnp.where(mask, row, 0.0), axis=1, keepdims=True)

    def follow(row, after):
        edge = (sub == seg_dev - 1) & (lane == 0)
        return column(lane == sub + 1, row) + column(edge, after)

    same = lane == sub
    pos = (lax.broadcasted_iota(jnp.int32, (1, rows), 1) + c * rows).astype(F32)
    own_col, own_end = column(same, own_row), follow(own_row, next_row)
    end_row = jnp.full((1, seg_dev), float(rows * n), F32)

    def belongs(first, last):
        return jnp.where((first <= pos) & (pos < last), 1.0, 0.0).astype(BF)

    member[0:seg_dev] = belongs(column(same, prev_row), follow(prev_row, own_row))
    member[seg_dev:2 * seg_dev] = belongs(own_col, own_end)
    member[2 * seg_dev:] = belongs(column(same, next_row), follow(next_row, end_row))

    def near_args(kind):
        return (near_out.at[kind, 0], near_out.at[kind, 1], near_in.at[kind],
                near_send.at[kind], near_recv.at[kind])

    for kind, load, rows_ref in ((0, cot_load, cot), (1, tok_load, tok)):
        load.wait()
        near_out[kind, 0] = mm(member[2 * seg_dev:], rows_ref[...]).astype(BF)
        near_out[kind, 1] = mm(member[0:seg_dev], rows_ref[...]).astype(BF)
        near_start(*near_args(kind))
    sum_cot = mm(member[seg_dev:2 * seg_dev], cot[...])
    sum_tok = mm(member[seg_dev:2 * seg_dev], tok[...])
    for kind in range(2):
        near_clear(near_in.at[kind])

    near_wait(*near_args(0))
    grad_sum = sum_cot + near_in[0, 0].astype(F32) + near_in[0, 1].astype(F32)
    head_out[...] = grad_sum[0:8]

    def g_rows(where):
        return gsum.at[pl.ds(pl.multiple_of(where * seg_dev, seg_dev), seg_dev)]

    def g_copy(o):
        return remote(g_rows(me), g_rows(me), g_send.at[o - 1], g_recv.at[o - 1],
                      dp=lax.rem(me + o, dp))

    def g_arrival(o):
        at = g_rows(lax.rem(me + dp - o, dp))
        return remote(at, at, g_send.at[o - 1], g_recv.at[o - 1], ctx=mate)

    gsum[pl.ds(pl.multiple_of(me * seg_dev, seg_dev), seg_dev)] = grad_sum.astype(BF)
    for o in range(1, dp):
        g_copy(o).start()

    def head_copy():
        return remote(head_out, head_in, head_send.at[0], head_recv.at[0], ctx=c - 1)

    @pl.when(has_prev)
    def _():
        head_copy().start()

    near_wait(*near_args(1))
    count = own_end - own_col
    pooled = (sum_tok + near_in[1, 0].astype(F32) + near_in[1, 1].astype(F32)) / count
    rms = jnp.sqrt(jnp.mean(pooled * pooled, axis=-1, keepdims=True) + 1e-06)
    normed = pooled / rms

    def spot(where):
        return gath.at[pl.ds(pl.multiple_of(where * seg_dev, seg_dev), seg_dev)]

    def hop(src_chip, sems, **where):
        at = 2 * src_chip + core
        return remote(spot(at), spot(at), sems.at[src_chip], gath_recv.at[at], **where)

    def go_right(src):
        return hop(src, right_send, ctx=c + 2)

    def go_left(src):
        return hop(src, left_send, ctx=c - 2)

    def go_pair(src):
        return hop(src, pair_send, ctx=mate)

    def arrival(where):
        return remote(spot(where), spot(where), right_send.at[0], gath_recv.at[where], ctx=mate)

    not_last, not_first = chip < chips - 1, chip > 0
    own_at = pl.ds(pl.multiple_of(c * seg_dev, seg_dev), seg_dev)
    gath[own_at] = (normed * gain[...]).astype(BF)

    @pl.when(not_last)
    def _():
        go_right(chip).start()

    @pl.when(not_first)
    def _():
        go_left(chip).start()

    go_pair(chip).start()

    def relay(s):
        @pl.when(chip - s >= 0)
        def _():
            arrival(c - 2 * s).wait_recv()

            @pl.when(not_last)
            def _():
                go_right(chip - s).start()

            go_pair(chip - s).start()

        @pl.when(chip + s < chips)
        def _():
            arrival(c + 2 * s).wait_recv()

            @pl.when(not_first)
            def _():
                go_left(chip + s).start()

            go_pair(chip + s).start()

    targets = [(b, j, q) for b in range(dp) for j in range(per_row) for q in range(parts)]

    def datt_copy(at):
        b, j, q = targets[at]
        to = me * per_row + j + q * heads
        return (b != me) | (to != c), remote(
            grads.at[pl.ds(b * seg_dev, seg_dev), pl.ds(j * HEAD, HEAD)], datt.at[own_at],
            datt_send.at[at], datt_recv.at[c], dp=b, ctx=to)

    def datt_arrival(src):
        at = pl.ds(pl.multiple_of(src * seg_dev, seg_dev), seg_dev)
        return (holder != me) | (src != c), remote(
            grads.at[pl.ds(0, seg_dev), pl.ds(0, HEAD)], datt.at[at],
            datt_send.at[src], datt_recv.at[src], ctx=mate)

    def own_datt():
        for o in range(1, dp):
            g_arrival(o).wait_recv()
        grads[...] = mm_nt(gsum[...], wo[...]).astype(BF)
        for at, (b, j, _) in enumerate(targets):
            away, copy = datt_copy(at)

            @pl.when(away)
            def _():
                copy.start()

            @pl.when(jnp.logical_not(away))
            def _():
                datt[own_at] = grads[b * seg_dev:(b + 1) * seg_dev, j * HEAD:(j + 1) * HEAD]

    for s in range(1, chips):
        relay(s)
        if s == min(2, chips - 1):
            own_datt()

    for o in range(1, dp):
        for i in range(3):
            w_arrival(o, i).wait_recv()
    for load in own_loads:
        load.wait()
    for other in range(chips):
        arrival(2 * other + 1 - core).wait_recv()

    step = 512 if segs % 512 == 0 else seg_dev

    def project(b, _):
        at = pl.ds(pl.multiple_of(b * step, step), step)
        qkv[at] = mm(gath[at], wcat[...]).astype(BF)
        return 0

    lax.fori_loop(0, segs // step, project, 0)
    for src in range(n):
        away, copy = datt_arrival(src)

        @pl.when(away)
        def _():
            copy.wait_recv()

    shifted = pltpu.roll(datt[...].astype(F32), segs - 1, 0)
    last = lax.broadcasted_iota(jnp.int32, (segs, HEAD), 0) == segs - 1
    datt[...] = jnp.where(last, 0.0, shifted).astype(BF)

    dkv[...] = jnp.zeros_like(dkv)
    if parts > 1:
        dqkv[...] = jnp.zeros_like(dqkv)
    block = 2 * seg_dev

    def attend(q_at, first, klen):
        q = qkv[q_at, 0:HEAD]
        key = qkv[0:klen, HEAD:2 * HEAD]
        value = qkv[0:klen, 2 * HEAD:]
        grad = datt[q_at]
        score = mm_nt(q, key) * scale
        allowed = (lax.broadcasted_iota(jnp.int32, (block, klen), 1)
                   <= lax.broadcasted_iota(jnp.int32, (block, klen), 0) + first)
        score = jnp.where(allowed, score, -1e30)
        peak = jnp.max(score, axis=-1, keepdims=True)
        expo = jnp.where(allowed, jnp.exp(score - peak), 0.0)
        probs = expo / jnp.sum(expo, axis=-1, keepdims=True)
        probs_b = probs.astype(BF)
        attended = mm(probs_b, value).astype(BF).astype(F32)
        delta = jnp.sum(grad.astype(F32) * attended, axis=-1, keepdims=True)
        dscore = (probs * (mm_nt(grad, value) - delta)).astype(BF)
        dqkv[q_at, 0:HEAD] = (mm(dscore, key) * scale).astype(BF)
        dkv[0:klen, 0:HEAD] += mm_tn(dscore, q)
        dkv[0:klen, HEAD:] += mm_tn(probs_b, grad)

    if parts > 1:
        per = segs // parts // block

        def body(b, _):
            first = pl.multiple_of((r * per + b) * block, block)
            attend(pl.ds(first, block), first, segs)
            return 0

        lax.fori_loop(0, per, body, 0)

    def sib_copy(t):
        return remote(part.at[1 - core, t], sib.at[t], sib_send.at[t], sib_recv.at[t], ctx=mate)

    def rs_copy(t):
        return remote(red.at[t], rs.at[chip], rs_send.at[t], rs_recv.at[chip], ctx=2 * t + core)

    def rs_arrival(t):
        return remote(red.at[t], rs.at[t], rs_send.at[t], rs_recv.at[t], ctx=mate)

    def term(t):
        at = slice(t * block, (t + 1) * block)
        dqkv[at, HEAD:2 * HEAD] = (dkv[at, 0:HEAD] * scale).astype(BF)
        dqkv[at, 2 * HEAD:] = dkv[at, HEAD:].astype(BF)
        both = mm_nt(dqkv[at], wcat[...])
        part[0, t] = both[0:seg_dev].astype(BF)
        part[1, t] = both[seg_dev:].astype(BF)
        sib_copy(t).start()

    def push(t):
        sib_copy(t).wait_recv()
        red[t] = (part[core, t].astype(F32) + sib[t].astype(F32)).astype(BF)

        @pl.when(chip != t)
        def _():
            rs_copy(t).start()

    for t in reversed(range(chips)):
        if parts == 1:
            attend(slice(t * block, (t + 1) * block), t * block, (t + 1) * block)
        term(t)
        if t + 1 < chips:
            push(t + 1)
    push(0)

    for other in range(chips):
        @pl.when(not_last & (other <= chip))
        def _():
            go_right(other).wait_send()

        @pl.when(not_first & (other >= chip))
        def _():
            go_left(other).wait_send()

        go_pair(other).wait_send()
        sib_copy(other).wait_send()
    for o in range(1, dp):
        for i in range(3):
            w_copy(o, i).wait_send()
        g_copy(o).wait_send()
    for at in range(len(targets)):
        away, copy = datt_copy(at)

        @pl.when(away)
        def _():
            copy.wait_send()

    @pl.when(has_prev)
    def _():
        head_copy().wait_send()

    @pl.when(has_next)
    def _():
        head_copy().wait_recv()

    @pl.when(jnp.logical_not(has_next))
    def _():
        head_in[...] = jnp.zeros_like(head_in)

    near_clear(seg_in)
    rolled = pltpu.roll(grad_sum, seg_dev - 1, 0)
    ends = lax.broadcasted_iota(jnp.int32, (seg_dev, width), 0) == seg_dev - 1
    dout = jnp.where(ends, head_in[0:1], rolled)

    dnormin = red[chip].astype(F32)
    for o in range(1, chips):
        t = lax.rem(chip + o, chips)
        rs_arrival(t).wait_recv()
        dnormin = dnormin + rs[t].astype(F32)

    scaled = dnormin * gain[...]
    dpooled = dout + (scaled - normed * jnp.mean(scaled * normed, axis=-1, keepdims=True)) / rms
    seg_out[...] = (dpooled / count).astype(BF)
    near_start(seg_out, seg_out, seg_in, seg_send, seg_recv)
    window[seg_dev:2 * seg_dev] = seg_out[...]
    for t in range(chips):
        @pl.when(chip != t)
        def _():
            rs_copy(t).wait_send()
    near_wait(seg_out, seg_out, seg_in, seg_send, seg_recv)
    window[0:seg_dev] = seg_in[0]
    window[2 * seg_dev:] = seg_in[1]


def per_device(tokens, starts, gain, w_query, w_key, w_value, w_out, cotangent):
    n, dp = lax.axis_size("ctx"), lax.axis_size("dp")
    chips = n // 2
    rows, width = tokens.shape[1:]
    seg_dev = starts.shape[1]
    segs = n * seg_dev
    dma = pltpu.SemaphoreType.DMA
    vmem = pltpu.VMEM
    scratch = [
        vmem((rows, width), BF), vmem((rows, width), BF),
        vmem((8, 128), jnp.int32), vmem((2, 8, 128), jnp.int32),
        vmem((2, 2, seg_dev, width), BF), vmem((2, 2, seg_dev, width), BF),
        vmem((8, width), F32), vmem((8, width), F32),
        vmem((segs, width), BF),
        vmem((width, 3 * HEAD), BF),
        vmem((dp * seg_dev, width), BF),
        vmem((dp * seg_dev, w_out.shape[0]), BF),
        vmem((segs, HEAD), BF),
        vmem((segs, 3 * HEAD), BF),
        vmem((segs, 3 * HEAD), BF),
        vmem((segs, 2 * HEAD), F32),
        vmem((2, chips, seg_dev, width), BF),
        vmem((chips, seg_dev, width), BF),
        vmem((chips, seg_dev, width), BF),
        vmem((chips, seg_dev, width), BF),
        vmem((seg_dev, width), BF),
        vmem((2, seg_dev, width), BF),
        dma((2,)), dma((2,)), dma((2,)), dma((2, 2)), dma((2, 2)), dma((1,)), dma((1,)), dma((2,)), dma((2,)),
        dma((dp - 1, 3)), dma((dp - 1, 3)), dma((3,)),
        dma((dp - 1,)), dma((dp - 1,)),
        dma((chips,)), dma((chips,)), dma((chips,)), dma((n,)), dma((n,)), dma((n,)),
        dma((chips,)), dma((chips,)), dma((chips,)), dma((chips,)),
    ]
    here, there = pl.BlockSpec(memory_space=pltpu.VMEM), pl.BlockSpec(memory_space=pl.ANY)
    window, member = pl.pallas_call(
        functools.partial(kernel, n, dp),
        out_shape=(
            jax.ShapeDtypeStruct((3 * seg_dev, width), BF),
            jax.ShapeDtypeStruct((3 * seg_dev, rows), BF),
        ),
        in_specs=[there, here, here, there, there, there, here, there],
        out_specs=(here, here),
        scratch_shapes=scratch,
        compiler_params=pltpu.CompilerParams(
            collective_id=0, has_side_effects=True, vmem_limit_bytes=56 * 1024 * 1024
        ),
    )(tokens, starts, gain[None], w_query, w_key, w_value, w_out, cotangent)
    return (cotangent[0].astype(F32) + mm_tn(member, window)).astype(BF)[None]


def solution(mesh):
    return jax.shard_map(
        per_device,
        mesh=mesh,
        in_specs=(
            P("dp", "ctx", None),
            P("dp", "ctx"),
            P(),
            P("dp", None),
            P("dp", None),
            P("dp", None),
            P("dp", None),
            P("dp", "ctx", None),
        ),
        out_specs=P("dp", "ctx", None),
        check_vma=False,
    )
```

```python
import functools
import math

import jax
import jax.numpy as jnp
from jax import lax
from jax.experimental import pallas as pl
from jax.experimental.pallas import tpu as pltpu
from jax.sharding import PartitionSpec as P

HEAD = 128
BF = jnp.bfloat16
F32 = jnp.float32


def dot(left, right, dims):
    return lax.dot_general(left, right, ((dims[0], dims[1]), ((), ())), preferred_element_type=F32)


def mm(left, right):
    return dot(left, right, ((1,), (0,)))


def mm_nt(left, right):
    return dot(left, right, ((1,), (1,)))


def mm_tn(left, right):
    return dot(left, right, ((0,), (0,)))


def remote(src, dst, send, recv, **where):
    return pltpu.make_async_remote_copy(
        src_ref=src, dst_ref=dst, send_sem=send, recv_sem=recv,
        device_id=where, device_id_type=pl.DeviceIdType.MESH,
    )


def kernel(
    n, dp,
    tok_hbm, starts, gain, wq, wk, wv, wo, cot_hbm, window, member,
    tok, cot, st_mine, st_near, near_out, near_in, head_out, head_in, gath, wcat, wout, grads, datt,
    qkv, dqkv, dkv, part, sib, red, rs, seg_out, seg_in,
    in_sem, st_send, st_recv, near_send, near_recv, head_send, head_recv, seg_send, seg_recv,
    w_send, w_recv, w_local, wo_send, wo_recv, wo_local, wo_fsend, wo_frecv,
    chip_send, pair_send, gath_recv, datt_send, datt_recv,
    sib_send, sib_recv, rs_send, rs_recv,
):
    me = lax.axis_index("dp")
    c = lax.axis_index("ctx")
    core = lax.rem(c, 2)
    chip = lax.div(c, 2)
    chips = n // 2
    mate = c + 1 - 2 * core
    rows, width = tok.shape
    seg_dev = starts.shape[1]
    segs = n * seg_dev
    w_rows, inner = wq.shape
    half = w_rows // 2
    heads = inner // HEAD
    parts = n // heads
    h = lax.rem(c, heads)
    r = lax.div(c, heads)
    scale = 1.0 / math.sqrt(HEAD)
    has_prev, has_next = c > 0, c < n - 1

    barrier = pltpu.get_barrier_semaphore()
    for o in range(1, n):
        pl.semaphore_signal(barrier, inc=1, device_id={"ctx": lax.rem(c + o, n)},
                            device_id_type=pl.DeviceIdType.MESH)
    for o in range(1, dp):
        pl.semaphore_signal(barrier, inc=1, device_id={"dp": lax.rem(me + o, dp)},
                            device_id_type=pl.DeviceIdType.MESH)

    def dp_rows(where, extra=0, size=w_rows):
        return pl.ds(pl.multiple_of(where * w_rows + extra, size), size)

    cot_load = pltpu.make_async_copy(cot_hbm.at[0], cot, in_sem.at[0])
    tok_load = pltpu.make_async_copy(tok_hbm.at[0], tok, in_sem.at[1])
    head_at = pl.ds(pl.multiple_of(h * HEAD, HEAD), HEAD)
    mats = (wq, wk, wv)
    own_loads = [
        pltpu.make_async_copy(mats[i].at[:, head_at], wcat.at[dp_rows(me), pl.ds(i * HEAD, HEAD)],
                              w_local.at[i])
        for i in range(3)
    ]
    own_loads.append(pltpu.make_async_copy(wo, wout.at[dp_rows(me)], wo_local.at[0]))
    cot_load.start()
    tok_load.start()
    for load in own_loads:
        load.start()
    st_mine[...] = jnp.zeros_like(st_mine)
    st_mine[0:1, 0:seg_dev] = starts[...]
    pl.semaphore_wait(barrier, n - 1 + dp - 1)

    def to_next(src, dst, send, recv):
        return remote(src, dst.at[0], send.at[0], recv.at[0], ctx=c + 1)

    def to_prev(src, dst, send, recv):
        return remote(src, dst.at[1], send.at[1], recv.at[1], ctx=c - 1)

    def near_start(src_next, src_prev, dst, send, recv):
        @pl.when(has_next)
        def _():
            to_next(src_next, dst, send, recv).start()

        @pl.when(has_prev)
        def _():
            to_prev(src_prev, dst, send, recv).start()

    def near_wait(src_next, src_prev, dst, send, recv):
        @pl.when(has_prev)
        def _():
            to_next(src_next, dst, send, recv).wait_recv()
            to_prev(src_prev, dst, send, recv).wait_send()

        @pl.when(has_next)
        def _():
            to_prev(src_prev, dst, send, recv).wait_recv()
            to_next(src_next, dst, send, recv).wait_send()

    def near_clear(dst):
        @pl.when(jnp.logical_not(has_prev))
        def _():
            dst[0] = jnp.zeros_like(dst[0])

        @pl.when(jnp.logical_not(has_next))
        def _():
            dst[1] = jnp.zeros_like(dst[1])

    near_start(st_mine, st_mine, st_near, st_send, st_recv)

    def wo_copy(o):
        return remote(wo.at[pl.ds(pl.multiple_of(core * half, half), half)],
                      wout.at[dp_rows(me, core * half, half)],
                      wo_send.at[o - 1], wo_recv.at[o - 1], dp=lax.rem(me + o, dp))

    def wo_arrival(o, which, sends, recvs):
        at = dp_rows(lax.rem(me + dp - o, dp), which * half, half)
        return remote(wout.at[at], wout.at[at], sends.at[o - 1], recvs.at[o - 1], ctx=mate)

    for o in range(1, dp):
        wo_copy(o).start()

    def w_copy(o, i):
        return remote(mats[i].at[:, head_at], wcat.at[dp_rows(me), pl.ds(i * HEAD, HEAD)],
                      w_send.at[o - 1, i], w_recv.at[o - 1, i], dp=lax.rem(me + o, dp))

    def w_arrival(o, i):
        src = lax.rem(me + dp - o, dp)
        return remote(mats[i].at[:, head_at], wcat.at[dp_rows(src), pl.ds(i * HEAD, HEAD)],
                      w_send.at[o - 1, i], w_recv.at[o - 1, i], dp=lax.rem(me + o, dp))

    near_wait(st_mine, st_mine, st_near, st_send, st_recv)
    own_row = starts[...].astype(F32)
    prev_row = jnp.where(has_prev, st_near[0, 0:1, 0:seg_dev].astype(F32), -1.0)
    next_row = jnp.where(has_next, st_near[1, 0:1, 0:seg_dev].astype(F32), float(rows * n))
    sub = lax.broadcasted_iota(jnp.int32, (seg_dev, seg_dev), 0)
    lane = lax.broadcasted_iota(jnp.int32, (seg_dev, seg_dev), 1)

    def column(mask, row):
        return jnp.sum(jnp.where(mask, row, 0.0), axis=1, keepdims=True)

    def follow(row, after):
        edge = (sub == seg_dev - 1) & (lane == 0)
        return column(lane == sub + 1, row) + column(edge, after)

    same = lane == sub
    pos = (lax.broadcasted_iota(jnp.int32, (1, rows), 1) + c * rows).astype(F32)
    own_col, own_end = column(same, own_row), follow(own_row, next_row)
    end_row = jnp.full((1, seg_dev), float(rows * n), F32)

    def belongs(first, last):
        return jnp.where((first <= pos) & (pos < last), 1.0, 0.0).astype(BF)

    member[0:seg_dev] = belongs(column(same, prev_row), follow(prev_row, own_row))
    member[seg_dev:2 * seg_dev] = belongs(own_col, own_end)
    member[2 * seg_dev:] = belongs(column(same, next_row), follow(next_row, end_row))

    def near_args(kind):
        return (near_out.at[kind, 0], near_out.at[kind, 1], near_in.at[kind],
                near_send.at[kind], near_recv.at[kind])

    for kind, load, rows_ref in ((0, cot_load, cot), (1, tok_load, tok)):
        load.wait()
        near_out[kind, 0] = mm(member[2 * seg_dev:], rows_ref[...]).astype(BF)
        near_out[kind, 1] = mm(member[0:seg_dev], rows_ref[...]).astype(BF)
        near_start(*near_args(kind))
    for o in range(1, dp):
        for i in range(3):
            w_copy(o, i).start()
    sum_cot = mm(member[seg_dev:2 * seg_dev], cot[...])
    sum_tok = mm(member[seg_dev:2 * seg_dev], tok[...])
    for kind in range(2):
        near_clear(near_in.at[kind])

    near_wait(*near_args(0))
    grad_sum = sum_cot + near_in[0, 0].astype(F32) + near_in[0, 1].astype(F32)
    head_out[...] = grad_sum[0:8]

    def head_copy():
        return remote(head_out, head_in, head_send.at[0], head_recv.at[0], ctx=c - 1)

    @pl.when(has_prev)
    def _():
        head_copy().start()

    near_wait(*near_args(1))
    count = own_end - own_col
    pooled = (sum_tok + near_in[1, 0].astype(F32) + near_in[1, 1].astype(F32)) / count
    rms = jnp.sqrt(jnp.mean(pooled * pooled, axis=-1, keepdims=True) + 1e-06)
    normed = pooled / rms

    def spot(where):
        return gath.at[pl.ds(pl.multiple_of(where * seg_dev, seg_dev), seg_dev)]

    def hop(src_chip, sems, **where):
        at = 2 * src_chip + core
        return remote(spot(at), spot(at), sems.at[src_chip], gath_recv.at[at], **where)

    def go_chip(o):
        to = lax.rem(chip + o, chips)
        return remote(spot(c), spot(c), chip_send.at[o - 1], gath_recv.at[c], ctx=2 * to + core)

    def go_pair(src):
        return hop(src, pair_send, ctx=mate)

    def arrival(where):
        return remote(spot(where), spot(where), pair_send.at[0], gath_recv.at[where], ctx=mate)

    own_at = pl.ds(pl.multiple_of(c * seg_dev, seg_dev), seg_dev)
    gath[own_at] = (normed * gain[...]).astype(BF)

    for o in range(1, chips):
        go_chip(o).start()
    go_pair(chip).start()

    def relay(s):
        @pl.when(chip - s >= 0)
        def _():
            arrival(c - 2 * s).wait_recv()
            go_pair(chip - s).start()

        @pl.when(chip + s < chips)
        def _():
            arrival(c + 2 * s).wait_recv()
            go_pair(chip + s).start()

    def datt_copy(o):
        to = lax.rem(c + o, n)
        cols = pl.ds(pl.multiple_of(lax.rem(to, heads) * HEAD, HEAD), HEAD)
        return remote(grads.at[:, cols], datt.at[own_at], datt_send.at[o - 1], datt_recv.at[o - 1],
                      ctx=to)

    def datt_arrival(o):
        src = lax.rem(c + n - o, n)
        at = pl.ds(pl.multiple_of(src * seg_dev, seg_dev), seg_dev)
        return remote(grads.at[:, head_at], datt.at[at], datt_send.at[o - 1], datt_recv.at[o - 1],
                      ctx=mate)

    def forward_wo():
        for o in range(1, dp):
            wo_arrival(o, core, wo_send, wo_recv).wait_recv()
            wo_arrival(o, core, wo_fsend, wo_frecv).start()

    def own_datt():
        own_loads[3].wait()
        for o in range(1, dp):
            wo_arrival(o, 1 - core, wo_fsend, wo_frecv).wait_recv()
        grads[...] = mm_nt(grad_sum.astype(BF), wout[...]).astype(BF)
        for o in range(1, n):
            datt_copy(o).start()
        datt[own_at] = grads[:, head_at]

    for s in range(1, chips):
        relay(s)
        if s == 1:
            forward_wo()
        if s == min(2, chips - 1):
            own_datt()

    for o in range(1, dp):
        for i in range(3):
            w_arrival(o, i).wait_recv()
    for load in own_loads[:3]:
        load.wait()
    for other in range(chips):
        arrival(2 * other + 1 - core).wait_recv()

    step = 512 if segs % 512 == 0 else seg_dev

    def project(b, _):
        at = pl.ds(pl.multiple_of(b * step, step), step)
        qkv[at] = mm(gath[at], wcat[...]).astype(BF)
        return 0

    lax.fori_loop(0, segs // step, project, 0)
    for o in range(1, n):
        datt_arrival(o).wait_recv()
    shifted = pltpu.roll(datt[...].astype(F32), segs - 1, 0)
    last = lax.broadcasted_iota(jnp.int32, (segs, HEAD), 0) == segs - 1
    datt[...] = jnp.where(last, 0.0, shifted).astype(BF)

    dkv[...] = jnp.zeros_like(dkv)
    if parts > 1:
        dqkv[...] = jnp.zeros_like(dqkv)
    block = 2 * seg_dev

    def attend(q_at, first, klen):
        q = qkv[q_at, 0:HEAD]
        key = qkv[0:klen, HEAD:2 * HEAD]
        value = qkv[0:klen, 2 * HEAD:]
        grad = datt[q_at]
        score = mm_nt(q, key) * scale
        allowed = (lax.broadcasted_iota(jnp.int32, (block, klen), 1)
                   <= lax.broadcasted_iota(jnp.int32, (block, klen), 0) + first)
        score = jnp.where(allowed, score, -1e30)
        peak = jnp.max(score, axis=-1, keepdims=True)
        expo = jnp.where(allowed, jnp.exp(score - peak), 0.0)
        probs = expo / jnp.sum(expo, axis=-1, keepdims=True)
        probs_b = probs.astype(BF)
        attended = mm(probs_b, value).astype(BF).astype(F32)
        delta = jnp.sum(grad.astype(F32) * attended, axis=-1, keepdims=True)
        dscore = (probs * (mm_nt(grad, value) - delta)).astype(BF)
        dqkv[q_at, 0:HEAD] = (mm(dscore, key) * scale).astype(BF)
        dkv[0:klen, 0:HEAD] += mm_tn(dscore, q)
        dkv[0:klen, HEAD:] += mm_tn(probs_b, grad)

    if parts > 1:
        per = segs // parts // block

        def body(b, _):
            first = pl.multiple_of((r * per + b) * block, block)
            attend(pl.ds(first, block), first, segs)
            return 0

        lax.fori_loop(0, per, body, 0)

    def sib_copy(t):
        return remote(part.at[1 - core, t], sib.at[t], sib_send.at[t], sib_recv.at[t], ctx=mate)

    def rs_copy(t):
        return remote(red.at[t], rs.at[chip], rs_send.at[t], rs_recv.at[chip], ctx=2 * t + core)

    def rs_arrival(t):
        return remote(red.at[t], rs.at[t], rs_send.at[t], rs_recv.at[t], ctx=mate)

    def term(t):
        at = slice(t * block, (t + 1) * block)
        dqkv[at, HEAD:2 * HEAD] = (dkv[at, 0:HEAD] * scale).astype(BF)
        dqkv[at, 2 * HEAD:] = dkv[at, HEAD:].astype(BF)
        both = mm_nt(dqkv[at], wcat[...])
        part[0, t] = both[0:seg_dev].astype(BF)
        part[1, t] = both[seg_dev:].astype(BF)
        sib_copy(t).start()

    def push(t):
        sib_copy(t).wait_recv()
        red[t] = (part[core, t].astype(F32) + sib[t].astype(F32)).astype(BF)

        @pl.when(chip != t)
        def _():
            rs_copy(t).start()

    for t in reversed(range(chips)):
        if parts == 1:
            attend(slice(t * block, (t + 1) * block), t * block, (t + 1) * block)
        term(t)
        if t + 1 < chips:
            push(t + 1)
    push(0)

    for other in range(chips):
        go_pair(other).wait_send()
        sib_copy(other).wait_send()
    for o in range(1, chips):
        go_chip(o).wait_send()
    for o in range(1, dp):
        for i in range(3):
            w_copy(o, i).wait_send()
        wo_copy(o).wait_send()
        wo_arrival(o, core, wo_fsend, wo_frecv).wait_send()
    for o in range(1, n):
        datt_copy(o).wait_send()

    @pl.when(has_prev)
    def _():
        head_copy().wait_send()

    @pl.when(has_next)
    def _():
        head_copy().wait_recv()

    @pl.when(jnp.logical_not(has_next))
    def _():
        head_in[...] = jnp.zeros_like(head_in)

    near_clear(seg_in)
    rolled = pltpu.roll(grad_sum, seg_dev - 1, 0)
    ends = lax.broadcasted_iota(jnp.int32, (seg_dev, width), 0) == seg_dev - 1
    dout = jnp.where(ends, head_in[0:1], rolled)

    dnormin = red[chip].astype(F32)
    for o in range(1, chips):
        t = lax.rem(chip + o, chips)
        rs_arrival(t).wait_recv()
        dnormin = dnormin + rs[t].astype(F32)

    scaled = dnormin * gain[...]
    dpooled = dout + (scaled - normed * jnp.mean(scaled * normed, axis=-1, keepdims=True)) / rms
    seg_out[...] = (dpooled / count).astype(BF)
    near_start(seg_out, seg_out, seg_in, seg_send, seg_recv)
    window[seg_dev:2 * seg_dev] = seg_out[...]
    for t in range(chips):
        @pl.when(chip != t)
        def _():
            rs_copy(t).wait_send()
    near_wait(seg_out, seg_out, seg_in, seg_send, seg_recv)
    window[0:seg_dev] = seg_in[0]
    window[2 * seg_dev:] = seg_in[1]


def per_device(tokens, starts, gain, w_query, w_key, w_value, w_out, cotangent):
    n, dp = lax.axis_size("ctx"), lax.axis_size("dp")
    chips = n // 2
    rows, width = tokens.shape[1:]
    seg_dev = starts.shape[1]
    segs = n * seg_dev
    dma = pltpu.SemaphoreType.DMA
    vmem = pltpu.VMEM
    scratch = [
        vmem((rows, width), BF), vmem((rows, width), BF),
        vmem((8, 128), jnp.int32), vmem((2, 8, 128), jnp.int32),
        vmem((2, 2, seg_dev, width), BF), vmem((2, 2, seg_dev, width), BF),
        vmem((8, width), F32), vmem((8, width), F32),
        vmem((segs, width), BF),
        vmem((width, 3 * HEAD), BF),
        vmem((dp * w_out.shape[0], width), BF),
        vmem((seg_dev, dp * w_out.shape[0]), BF),
        vmem((segs, HEAD), BF),
        vmem((segs, 3 * HEAD), BF),
        vmem((segs, 3 * HEAD), BF),
        vmem((segs, 2 * HEAD), F32),
        vmem((2, chips, seg_dev, width), BF),
        vmem((chips, seg_dev, width), BF),
        vmem((chips, seg_dev, width), BF),
        vmem((chips, seg_dev, width), BF),
        vmem((seg_dev, width), BF),
        vmem((2, seg_dev, width), BF),
        dma((2,)), dma((2,)), dma((2,)), dma((2, 2)), dma((2, 2)), dma((1,)), dma((1,)), dma((2,)), dma((2,)),
        dma((dp - 1, 3)), dma((dp - 1, 3)), dma((3,)),
        dma((dp - 1,)), dma((dp - 1,)), dma((1,)), dma((dp - 1,)), dma((dp - 1,)),
        dma((chips,)), dma((chips,)), dma((n,)), dma((n - 1,)), dma((n - 1,)),
        dma((chips,)), dma((chips,)), dma((chips,)), dma((chips,)),
    ]
    here, there = pl.BlockSpec(memory_space=pltpu.VMEM), pl.BlockSpec(memory_space=pl.ANY)
    window, member = pl.pallas_call(
        functools.partial(kernel, n, dp),
        out_shape=(
            jax.ShapeDtypeStruct((3 * seg_dev, width), BF),
            jax.ShapeDtypeStruct((3 * seg_dev, rows), BF),
        ),
        in_specs=[there, here, here, there, there, there, there, there],
        out_specs=(here, here),
        scratch_shapes=scratch,
        compiler_params=pltpu.CompilerParams(
            collective_id=0, has_side_effects=True, vmem_limit_bytes=56 * 1024 * 1024
        ),
    )(tokens, starts, gain[None], w_query, w_key, w_value, w_out, cotangent)
    return (cotangent[0].astype(F32) + mm_tn(member, window)).astype(BF)[None]


def solution(mesh):
    return jax.shard_map(
        per_device,
        mesh=mesh,
        in_specs=(
            P("dp", "ctx", None),
            P("dp", "ctx"),
            P(),
            P("dp", None),
            P("dp", None),
            P("dp", None),
            P("dp", None),
            P("dp", "ctx", None),
        ),
        out_specs=P("dp", "ctx", None),
        check_vma=False,
    )
```
